128 devices in a mesh: tm: 4 (over y_lo, core), space: 32 (over y_hi, z, x).
Axes of the slice: x: 4, y: 4 (y_hi: 2, y_lo: 2; y = y_hi * 2 + y_lo), z: 4, core: 2. Of those that a mesh axis runs over, the one named last changes fastest.
Arguments:
- space_query: bfloat16 [1, 16, 1024, 4096], P(None, 'tm', 'space'), may hold values from -28 to 28
- space_key: bfloat16 [1, 16, 1024, 4096], P(None, 'tm', 'space'), may hold values from -28 to 28
- space_value: bfloat16 [1, 16, 1024, 4096], P(None, 'tm', 'space'), may hold values from -6 to 6
- space_grad: bfloat16 [1, 16, 1024, 4096], P(None, 'tm', 'space'), may hold values from -6 to 6
- time_query: bfloat16 [1, 16, 1024, 4096], P(None, 'tm', 'space'), may hold values from -28 to 28
- time_key: bfloat16 [1, 16, 1024, 4096], P(None, 'tm', 'space'), may hold values from -28 to 28
- time_value: bfloat16 [1, 16, 1024, 4096], P(None, 'tm', 'space'), may hold values from -6 to 6
- time_grad: bfloat16 [1, 16, 1024, 4096], P(None, 'tm', 'space'), may hold values from -6 to 6
Outputs:
- space_dquery: bfloat16 [1, 16, 1024, 4096], P(None, 'tm', 'space')
- space_dkey: bfloat16 [1, 16, 1024, 4096], P(None, 'tm', 'space')
- space_dvalue: bfloat16 [1, 16, 1024, 4096], P(None, 'tm', 'space')
- time_dquery: bfloat16 [1, 16, 1024, 4096], P(None, 'tm', 'space')
- time_dkey: bfloat16 [1, 16, 1024, 4096], P(None, 'tm', 'space')
- time_dvalue: bfloat16 [1, 16, 1024, 4096], P(None, 'tm', 'space')
The draws below stay inside these ranges and needn't reach their ends.
All inputs are finite; a program needn't handle non-finite values.
Results may differ from the reference program's by a relative error of at most 0.02.
Values may be sent and summed in bfloat16 or wider, within the bound.
No kernel may reach another device: no remote copies, remote signals or barrier semaphores. Data moves between devices by JAX's collectives and lax.ppermute only.
A program may use at most 128 MiB of HBM per device.

```python
import jax
import jax.numpy as jnp
from jax import lax

HEADS = 32
HEAD_DIM = 128
D = 4096
FRAMES = 16
POS = 1024
CLIPS = 1


def aligned_pair(key, rate):
    key_query, key_key, key_pick, key_size = jax.random.split(key, 4)
    shape = (CLIPS, FRAMES, POS, D)
    normal_query = jnp.clip(jax.random.normal(key_query, shape, jnp.float32), -6.0, 6.0)
    normal_key = jnp.clip(jax.random.normal(key_key, shape, jnp.float32), -6.0, 6.0)
    base_query = normal_query
    base_key = normal_key
    small = (CLIPS, FRAMES, POS, 1)
    frame_index = lax.broadcasted_iota(jnp.int32, small, 1)
    position_index = lax.broadcasted_iota(jnp.int32, small, 2)
    picked = (jax.random.uniform(key_pick, small, jnp.float32) < rate) & (frame_index >= 1) & (position_index < POS - 1)
    strength = jax.random.uniform(key_size, small, jnp.float32, 3.4, 4.6)
    strong = strength * base_key
    query_rows = jnp.where(picked, strong, base_query)
    key_rows = jnp.where(picked, strong, base_key)
    picked_next = jnp.roll(picked, 1, axis=2)
    key_rows = jnp.where(picked_next & ~picked, 0.99 * jnp.roll(strong, 1, axis=2), key_rows)
    picked_prior = jnp.roll(picked, -1, axis=1)
    key_rows = jnp.where(picked_prior & ~picked & ~picked_next, 0.992 * jnp.roll(strong, -1, axis=1), key_rows)
    return (query_rows, key_rows)


def draw_space_query(key, part):
    pair = aligned_pair(jax.random.fold_in(key, 1), 0.0)
    return pair[0].astype(jnp.bfloat16)


def draw_space_key(key, part):
    pair = aligned_pair(jax.random.fold_in(key, 1), 0.0)
    return pair[1].astype(jnp.bfloat16)


def draw_time_query(key, part):
    pair = aligned_pair(jax.random.fold_in(key, 2), 0.0)
    return pair[0].astype(jnp.bfloat16)


def draw_time_key(key, part):
    pair = aligned_pair(jax.random.fold_in(key, 2), 0.0)
    return pair[1].astype(jnp.bfloat16)


def block_levels(stream_key, extent, cuts, low, largest):
    loudness = 1.0
    for dim, shards_of in cuts:
        draws = jax.random.uniform(jax.random.fold_in(jax.random.fold_in(stream_key, 6), dim), (shards_of,), jnp.float32, low / len(cuts), largest / len(cuts))
        loudness = loudness * jnp.repeat(jnp.exp(draws), extent[dim] // shards_of).reshape((-1,) + (1,) * (len(extent) - 1 - dim))
    return loudness


def gaussian(rng, shape, scale, most, cuts=(), kind=jnp.bfloat16):
    values = jax.random.normal(rng, shape, jnp.float32) * scale
    if len(cuts) > 0:
        values = block_levels(rng, shape, cuts, -0.22, 0.18) * values
    return jnp.clip(values, min=-most, max=most).astype(kind)


def setup_inputs(seed: int = 0) -> dict:
    splits = jax.random.split(jax.random.key(seed), 9)
    space_query = draw_space_query(jax.random.fold_in(splits[8], 71), 0)
    space_key = draw_space_key(jax.random.fold_in(splits[8], 71), 0)
    space_value = gaussian(splits[2], (CLIPS, FRAMES, POS, D), 1.0, 6.0, ((1, 4), (2, 32)))
    space_grad = gaussian(splits[3], (CLIPS, FRAMES, POS, D), 1.0, 6.0, ((1, 4), (2, 32)))
    time_query = draw_time_query(jax.random.fold_in(splits[8], 71), 0)
    time_key = draw_time_key(jax.random.fold_in(splits[8], 71), 0)
    time_value = gaussian(splits[6], (CLIPS, FRAMES, POS, D), 1.0, 6.0, ((1, 4), (2, 32)))
    time_grad = gaussian(splits[7], (CLIPS, FRAMES, POS, D), 1.0, 6.0, ((1, 4), (2, 32)))
    return {"space_query": space_query, "space_key": space_key, "space_value": space_value, "space_grad": space_grad, "time_query": time_query, "time_key": time_key, "time_value": time_value, "time_grad": time_grad}


def to_low(values):
    rounded = values.astype(jnp.bfloat16)
    rounded = lax.optimization_barrier(rounded)
    return rounded.astype(jnp.float32)

def spatial_frame(pieces):
    query_rows, key_rows, value_rows, grad_rows = pieces
    clip_count, positions, width = query_rows.shape
    shape_heads = (clip_count, positions, HEADS, HEAD_DIM)
    queries = query_rows.astype(jnp.float32).reshape(shape_heads)
    keyset = key_rows.astype(jnp.float32).reshape(shape_heads)
    valueset = value_rows.astype(jnp.float32).reshape(shape_heads)
    gradset = grad_rows.astype(jnp.float32).reshape(shape_heads)
    score_scale = 1.0 / jnp.sqrt(jnp.float32(HEAD_DIM))
    scores = jnp.einsum('cqhd,ckhd->chqk', queries, keyset) * score_scale
    row_peak = lax.optimization_barrier(jnp.max(scores, axis=-1, keepdims=True))
    exponent = jnp.exp(scores - row_peak)
    probs = exponent / lax.optimization_barrier(jnp.sum(exponent, axis=-1, keepdims=True))
    weights_low = to_low(probs)
    output = jnp.einsum('chqk,ckhd->cqhd', weights_low, valueset)
    row_delta = lax.optimization_barrier(jnp.sum(gradset * output, axis=-1))
    prob_grad = jnp.einsum('cqhd,ckhd->chqk', gradset, valueset)
    score_grad = to_low(probs * (prob_grad - jnp.transpose(row_delta, (0, 2, 1))[..., None]))
    dquery = jnp.einsum('chqk,ckhd->cqhd', score_grad, keyset) * score_scale
    dkey = jnp.einsum('chqk,cqhd->ckhd', score_grad, queries) * score_scale
    dvalue = jnp.einsum('chqk,cqhd->ckhd', weights_low, gradset)
    return tuple((item.reshape(clip_count, positions, width).astype(jnp.bfloat16) for item in (dquery, dkey, dvalue)))

def temporal_all(query_rows, key_rows, value_rows, grad_rows):
    clip_count, frame_count, positions, width = query_rows.shape
    shape_heads = (clip_count, frame_count, positions, HEADS, HEAD_DIM)
    queries = query_rows.astype(jnp.float32).reshape(shape_heads)
    keyset = key_rows.astype(jnp.float32).reshape(shape_heads)
    valueset = value_rows.astype(jnp.float32).reshape(shape_heads)
    gradset = grad_rows.astype(jnp.float32).reshape(shape_heads)
    score_scale = 1.0 / jnp.sqrt(jnp.float32(HEAD_DIM))
    scores = jnp.einsum('cfphd,cgphd->cphfg', queries, keyset) * score_scale
    frame_query = lax.broadcasted_iota(jnp.int32, (frame_count, frame_count), 0)
    frame_key = lax.broadcasted_iota(jnp.int32, (frame_count, frame_count), 1)
    allowed = frame_key <= frame_query
    scores = jnp.where(allowed, scores, jnp.float32(-1e+30))
    row_peak = lax.optimization_barrier(jnp.max(scores, axis=-1, keepdims=True))
    exponent = jnp.where(allowed, jnp.exp(scores - row_peak), jnp.float32(0.0))
    probs = exponent / lax.optimization_barrier(jnp.sum(exponent, axis=-1, keepdims=True))
    weights_low = to_low(probs)
    output = jnp.einsum('cphfg,cgphd->cfphd', weights_low, valueset)
    row_delta = lax.optimization_barrier(jnp.sum(gradset * output, axis=-1))
    prob_grad = jnp.einsum('cfphd,cgphd->cphfg', gradset, valueset)
    delta_moved = jnp.transpose(row_delta, (0, 2, 3, 1))[..., None]
    score_grad = to_low(probs * (prob_grad - delta_moved))
    dquery = jnp.einsum('cphfg,cgphd->cfphd', score_grad, keyset) * score_scale
    dkey = jnp.einsum('cphfg,cfphd->cgphd', score_grad, queries) * score_scale
    dvalue = jnp.einsum('cphfg,cfphd->cgphd', weights_low, gradset)
    return tuple((item.reshape(clip_count, frame_count, positions, width).astype(jnp.bfloat16) for item in (dquery, dkey, dvalue)))

def reference(space_query, space_key, space_value, space_grad, time_query, time_key, time_value, time_grad):
    moved = tuple((jnp.transpose(item, (1, 0, 2, 3)) for item in (space_query, space_key, space_value, space_grad)))
    space_out = lax.map(spatial_frame, moved)
    space_dquery, space_dkey, space_dvalue = tuple((jnp.transpose(item, (1, 0, 2, 3)) for item in space_out))
    time_dquery, time_dkey, time_dvalue = temporal_all(time_query, time_key, time_value, time_grad)
    return (space_dquery, space_dkey, space_dvalue, time_dquery, time_dkey, time_dvalue)
```

```python
import functools
import math

import jax
import jax.numpy as jnp
from jax import lax
from jax.experimental import pallas as pl
from jax.experimental.pallas import tpu as pltpu
from jax.sharding import PartitionSpec as P

HEAD_DIM = 128
SCALE = 1.0 / math.sqrt(HEAD_DIM)
LOG2E = 1.0 / math.log(2.0)


def dot(a, b, contract):
    return lax.dot_general(a, b, (contract, ((), ())), preferred_element_type=jnp.float32)


def pack_kernel(*refs):
    *ins, out = refs
    heads = out.shape[0]
    for a, ref in enumerate(ins):
        for h in range(heads):
            out[h, 0, a] = ref[0, :, h * HEAD_DIM : (h + 1) * HEAD_DIM]


def pack_heads(*arrays):
    frames, positions, width = arrays[0].shape
    heads = width // HEAD_DIM
    count = len(arrays)
    return pl.pallas_call(
        pack_kernel,
        grid=(frames,),
        in_specs=[pl.BlockSpec((1, positions, width), lambda f: (f, 0, 0))] * count,
        out_specs=pl.BlockSpec(
            (heads, 1, count, positions, HEAD_DIM), lambda f: (0, f, 0, 0, 0)
        ),
        out_shape=jax.ShapeDtypeStruct(
            (heads, frames, count, positions, HEAD_DIM), arrays[0].dtype
        ),
        name="pack_heads",
    )(*arrays)


def unpack_kernel(ref, *outs):
    heads = ref.shape[0]
    for a, out in enumerate(outs):
        for h in range(heads):
            out[0, :, h * HEAD_DIM : (h + 1) * HEAD_DIM] = ref[h, 0, a]


def unpack_heads(array):
    heads, frames, count, positions, _ = array.shape
    width = heads * HEAD_DIM
    return pl.pallas_call(
        unpack_kernel,
        grid=(frames,),
        in_specs=[
            pl.BlockSpec((heads, 1, count, positions, HEAD_DIM), lambda f: (0, f, 0, 0, 0))
        ],
        out_specs=[pl.BlockSpec((1, positions, width), lambda f: (f, 0, 0))] * count,
        out_shape=[jax.ShapeDtypeStruct((frames, positions, width), array.dtype)] * count,
        name="unpack_heads",
    )(array)


def spatial_kernel(block, ref, out):
    parts, _, _, rows, _ = ref.shape
    total = parts * rows
    query, key, value, grad = (ref[:, 0, a].reshape(total, HEAD_DIM) for a in range(4))
    key_t = key.T
    dkey = dvalue = None
    for start in range(0, total, block):
        q = query[start : start + block]
        g = grad[start : start + block]
        scores = dot(key, q, ((1,), (1,)))
        peak = jnp.max(scores, axis=0, keepdims=True)
        e = jnp.exp2((scores - peak) * (SCALE * LOG2E))
        pgrad = dot(value, g, ((1,), (1,)))
        probs = e * (1.0 / jnp.sum(e, axis=0, keepdims=True))
        weights = probs.astype(jnp.bfloat16)
        term = probs * pgrad
        delta = jnp.sum(term, axis=0, keepdims=True)
        sgrad = (term - probs * delta).astype(jnp.bfloat16)
        dq = dot(key_t, sgrad, ((1,), (0,))).T * SCALE
        out[start // rows : (start + block) // rows, 0, 0] = dq.astype(out.dtype).reshape(
            block // rows, rows, HEAD_DIM
        )
        dk = dot(sgrad, q, ((1,), (0,)))
        dv = dot(weights, g, ((1,), (0,)))
        dkey = dk if dkey is None else dkey + dk
        dvalue = dv if dvalue is None else dvalue + dv
    out[:, 0, 1] = (dkey * SCALE).astype(out.dtype).reshape(parts, rows, HEAD_DIM)
    out[:, 0, 2] = dvalue.astype(out.dtype).reshape(parts, rows, HEAD_DIM)


def spatial_grads(array):
    parts, frames, _, rows, _ = array.shape
    return pl.pallas_call(
        functools.partial(spatial_kernel, min(256, parts * rows)),
        grid=(frames,),
        in_specs=[pl.BlockSpec((parts, 1, 4, rows, HEAD_DIM), lambda f: (0, f, 0, 0, 0))],
        out_specs=pl.BlockSpec((parts, 1, 3, rows, HEAD_DIM), lambda f: (0, f, 0, 0, 0)),
        out_shape=jax.ShapeDtypeStruct((parts, frames, 3, rows, HEAD_DIM), array.dtype),
        compiler_params=pltpu.CompilerParams(vmem_limit_bytes=48 * 1024 * 1024),
        name="spatial_grads",
    )(array)


GROUP = 16
NEVER = -1e30


def ship_kernel(query, key, value, grad, same, other, sems):
    member = lax.axis_index("tm")
    chip, core = member // 2, member % 2
    width = same.shape[-1]

    def copy_all(first, second, row):
        copies = []
        for half, out in ((core, same), (1 - core, other)):
            columns = pl.ds(pl.multiple_of(half * width, width), width)
            for a, ref in enumerate((first, second)):
                copies.append(
                    pltpu.make_async_copy(
                        ref.at[:, pl.ds(row, GROUP), columns], out.at[a], sems.at[len(copies)]
                    )
                )
        for copy in copies:
            copy.start()
        for copy in copies:
            copy.wait()

    @pl.when(chip == 0)
    def _():
        copy_all(key, value, 0)

    @pl.when(chip == 1)
    def _():
        copy_all(query, grad, GROUP)


def ship_pack(query, key, value, grad):
    frames, _, width = query.shape
    shape = jax.ShapeDtypeStruct((2, frames, GROUP, width // 2), query.dtype)
    return pl.pallas_call(
        ship_kernel,
        in_specs=[pl.BlockSpec(memory_space=pl.ANY)] * 4,
        out_specs=[pl.BlockSpec(memory_space=pl.ANY)] * 2,
        out_shape=[shape, shape],
        scratch_shapes=[pltpu.SemaphoreType.DMA((4,))],
        name="ship_pack",
    )(query, key, value, grad)


def swap_kernel(*refs):
    *ins, out, sems = refs
    core = lax.axis_index("tm") % 2
    width = out.shape[-1]
    columns = pl.ds(pl.multiple_of((1 - core) * width, width), width)
    copies = [
        pltpu.make_async_copy(ref.at[:, :, columns], out.at[a], sems.at[a])
        for a, ref in enumerate(ins)
    ]
    for copy in copies:
        copy.start()
    for copy in copies:
        copy.wait()


def swap_pack(*arrays):
    frames, positions, width = arrays[0].shape
    count = len(arrays)
    return pl.pallas_call(
        swap_kernel,
        in_specs=[pl.BlockSpec(memory_space=pl.ANY)] * count,
        out_specs=pl.BlockSpec(memory_space=pl.ANY),
        out_shape=jax.ShapeDtypeStruct((count, frames, positions, width // 2), arrays[0].dtype),
        scratch_shapes=[pltpu.SemaphoreType.DMA((count,))],
        name="swap_pack",
    )(*arrays)


def frame_mask(core, chip_frames, causal):
    rows = chip_frames * GROUP
    half = chip_frames // 2
    key_row = lax.broadcasted_iota(jnp.int32, (rows, rows), 0)
    query_row = lax.broadcasted_iota(jnp.int32, (rows, rows), 1)
    same = key_row % GROUP == query_row % GROUP
    key_frame = (key_row // GROUP + core * half) % chip_frames
    query_frame = (query_row // GROUP + core * half) % chip_frames
    return same & ((key_frame <= query_frame) | jnp.logical_not(causal))


def gather_rows(own, other, row, columns):
    rows = pl.ds(row, GROUP)
    return jnp.concatenate(
        [
            own[:, rows, columns].reshape(-1, HEAD_DIM),
            other[:, rows, columns].reshape(-1, HEAD_DIM),
        ],
        axis=0,
    )


def block_stats(mask, query, key, value, grad):
    scores = dot(key, query, ((1,), (1,))) * (SCALE * LOG2E)
    scores = jnp.where(mask, scores, NEVER)
    peak = jnp.max(scores, axis=0, keepdims=True)
    e = jnp.exp2(scores - peak)
    pgrad = dot(value, grad, ((1,), (1,)))
    return (
        (scores, pgrad),
        (peak, jnp.sum(e, axis=0, keepdims=True), jnp.sum(e * pgrad, axis=0, keepdims=True)),
    )


def block_grads(products, stats, more, query, key, grad):
    scores, pgrad = products
    peak = jnp.maximum(stats[0], more[0])
    own_scale, more_scale = jnp.exp2(stats[0] - peak), jnp.exp2(more[0] - peak)
    inverse = 1.0 / (stats[1] * own_scale + more[1] * more_scale)
    delta = (stats[2] * own_scale + more[2] * more_scale) * inverse
    probs = jnp.exp2(scores - peak) * inverse
    weights = probs.astype(jnp.bfloat16)
    sgrad = (probs * (pgrad - delta)).astype(jnp.bfloat16)
    dquery = dot(sgrad, key, ((0,), (0,))) * SCALE
    dkey = dot(sgrad, query, ((1,), (0,))) * SCALE
    dvalue = dot(weights, grad, ((1,), (0,)))
    return dquery, dkey, dvalue


def stats_kernel(place, query, key, value, grad, swapped, same, other, out):
    core, chip = place[0], place[1]
    frames = query.shape[0]
    mask = frame_mask(core, 2 * frames, chip == 1)
    for h in range(query.shape[-1] // HEAD_DIM):
        columns = pl.ds(h * HEAD_DIM, HEAD_DIM)
        own = [
            gather_rows(ref, swapped.at[a], GROUP, columns)
            for a, ref in enumerate((query, key, value, grad))
        ]
        sent = [gather_rows(same.at[a], other.at[a], 0, columns) for a in range(2)]
        q = jnp.where(chip == 0, sent[0], own[0])
        g = jnp.where(chip == 0, sent[1], own[3])
        _, stats = block_stats(mask, q, own[1], own[2], g)
        out[h] = jnp.concatenate(stats + (jnp.zeros((5, stats[0].shape[1]), jnp.float32),), axis=0)


def grads_kernel(
    place, query, key, value, grad, swapped, same, other, far, mine, theirs, back, back_other
):
    core, chip = place[0], place[1]
    frames = query.shape[0]
    causal = frame_mask(core, 2 * frames, True)
    cross = frame_mask(core, 2 * frames, False)
    first = chip == 0
    for h in range(query.shape[-1] // HEAD_DIM):
        columns = pl.ds(h * HEAD_DIM, HEAD_DIM)
        early, late = (
            [
                gather_rows(ref, swapped.at[a], row, columns)
                for a, ref in enumerate((query, key, value, grad))
            ]
            for row in (0, GROUP)
        )
        sent = [gather_rows(same.at[a], other.at[a], 0, columns) for a in range(2)]
        crossed = [
            jnp.where(first, sent[0], early[0]),
            jnp.where(first, late[1], sent[0]),
            jnp.where(first, late[2], sent[1]),
            jnp.where(first, sent[1], early[3]),
        ]
        received = tuple(far[h, i : i + 1] for i in range(3))
        none = (
            jnp.full_like(received[0], NEVER),
            jnp.zeros_like(received[1]),
            jnp.zeros_like(received[2]),
        )
        early_products, early_stats = block_stats(causal, *early)
        late_products, late_stats = block_stats(causal, *late)
        cross_products, cross_stats = block_stats(cross, *crossed)

        def choose(when_first, when_second):
            return tuple(jnp.where(first, a, b) for a, b in zip(when_first, when_second))

        early_out = block_grads(
            early_products, early_stats, choose(none, cross_stats), early[0], early[1], early[3]
        )
        late_out = block_grads(
            late_products, late_stats, choose(none, received), late[0], late[1], late[3]
        )
        cross_out = block_grads(
            cross_products,
            cross_stats,
            choose(received, early_stats),
            crossed[0],
            crossed[1],
            crossed[3],
        )
        zero = jnp.zeros_like(cross_out[0])
        early_out = (early_out[0] + jnp.where(first, zero, cross_out[0]),) + early_out[1:]
        late_out = (late_out[0],) + tuple(
            a + jnp.where(first, b, zero) for a, b in zip(late_out[1:], cross_out[1:])
        )
        back_out = (
            jnp.where(first, cross_out[0], cross_out[1]),
            jnp.where(first, zero, cross_out[2]),
        )

        def place_rows(own, others, a, row, values):
            values = values.astype(jnp.bfloat16).reshape(2, frames, GROUP, HEAD_DIM)
            own[a, :, pl.ds(row, GROUP), columns] = values[0]
            others[a, :, pl.ds(row, GROUP), columns] = values[1]

        for a in range(3):
            place_rows(mine, theirs, a, 0, early_out[a])
            place_rows(mine, theirs, a, GROUP, late_out[a])
        for a in range(2):
            place_rows(back, back_other, a, 0, back_out[a])


def finish_kernel(place, mine, swapped, back, back_swapped, dquery, dkey, dvalue):
    first = place[1] == 0

    def write(ref, far):
        early, late = pl.ds(0, GROUP), pl.ds(GROUP, GROUP)
        zero = jnp.zeros(far.shape[1:], jnp.float32)
        far_first, far_second = far[0].astype(jnp.float32), far[1].astype(jnp.float32)

        def added(a, rows, more):
            return (ref[a, :, rows].astype(jnp.float32) + more).astype(jnp.bfloat16)

        dquery[:, early] = ref[0, :, early]
        dquery[:, late] = added(0, late, jnp.where(first, zero, far_first))
        dkey[:, early] = added(1, early, jnp.where(first, far_first, zero))
        dkey[:, late] = ref[1, :, late]
        dvalue[:, early] = added(2, early, jnp.where(first, far_second, zero))
        dvalue[:, late] = ref[2, :, late]

    @pl.when(pl.program_id(0) == 0)
    def _():
        write(mine, back)

    @pl.when(pl.program_id(0) == 1)
    def _():
        write(swapped, back_swapped)


STEPS = 4


def temporal_grads(query, key, value, grad):
    frames, positions, width = query.shape
    half = width // 2
    block = half // STEPS
    heads = half // HEAD_DIM
    step_heads = heads // STEPS
    member = lax.axis_index("tm")
    place = jnp.stack([member % 2, member // 2])
    chips = [(t, t ^ 2) for t in range(4)]
    cores = [(t, t ^ 1) for t in range(4)]
    arrays = (query, key, value, grad)

    ship_same, ship_other = ship_pack(*arrays)
    ship_other = lax.ppermute(ship_other, "tm", chips)
    ship_same = lax.ppermute(ship_same, "tm", chips)
    swapped = lax.ppermute(swap_pack(*arrays), "tm", cores)
    ship_other = lax.ppermute(ship_other, "tm", cores)

    own_spec = pl.BlockSpec((frames, positions, block), lambda j, p: (0, 0, p[0] * STEPS + j))

    def half_spec(count, rows):
        return pl.BlockSpec((count, frames, rows, block), lambda j, p: (0, 0, 0, j))

    stats_spec = pl.BlockSpec((step_heads, 8, 2 * frames * GROUP), lambda j, p: (j, 0, 0))
    inputs = [own_spec] * 4 + [half_spec(4, positions), half_spec(2, GROUP), half_spec(2, GROUP)]
    operands = arrays + (swapped, ship_same, ship_other)
    stats = pl.pallas_call(
        stats_kernel,
        grid_spec=pltpu.PrefetchScalarGridSpec(
            num_scalar_prefetch=1, grid=(STEPS,), in_specs=inputs, out_specs=stats_spec
        ),
        out_shape=jax.ShapeDtypeStruct((heads, 8, 2 * frames * GROUP), jnp.float32),
        name="temporal_stats",
    )(place, *operands)
    far = lax.ppermute(stats, "tm", chips)

    def half_shape(count, rows):
        return jax.ShapeDtypeStruct((count, frames, rows, half), query.dtype)

    mine, theirs, back, back_other = pl.pallas_call(
        grads_kernel,
        grid_spec=pltpu.PrefetchScalarGridSpec(
            num_scalar_prefetch=1,
            grid=(STEPS,),
            in_specs=inputs + [stats_spec],
            out_specs=[half_spec(3, positions)] * 2 + [half_spec(2, GROUP)] * 2,
        ),
        out_shape=[half_shape(3, positions)] * 2 + [half_shape(2, GROUP)] * 2,
        name="temporal_grads",
    )(place, *operands, far)
    return place, mine, theirs, back, back_other


def temporal_finish(place, mine, theirs, back, back_other):
    _, frames, positions, half = mine.shape
    block = half // STEPS
    chips = [(t, t ^ 2) for t in range(4)]
    cores = [(t, t ^ 1) for t in range(4)]
    back_other = lax.ppermute(back_other, "tm", chips)
    back = lax.ppermute(back, "tm", chips)
    swapped = lax.ppermute(theirs, "tm", cores)
    back_other = lax.ppermute(back_other, "tm", cores)

    def spec(which, count, rows):
        return pl.BlockSpec(
            (count, frames, rows, block),
            (lambda i, j, p: (0, 0, 0, jnp.where(i == 0, j, STEPS - 1)))
            if which == 0
            else (lambda i, j, p: (0, 0, 0, jnp.where(i == 0, 0, j))),
        )

    out_spec = pl.BlockSpec(
        (frames, positions, block),
        lambda i, j, p: (0, 0, jnp.where(i == 0, p[0], 1 - p[0]) * STEPS + j),
    )
    out_shape = jax.ShapeDtypeStruct((frames, positions, 2 * half), mine.dtype)
    return pl.pallas_call(
        finish_kernel,
        grid_spec=pltpu.PrefetchScalarGridSpec(
            num_scalar_prefetch=1,
            grid=(2, STEPS),
            in_specs=[spec(0, 3, positions), spec(1, 3, positions), spec(0, 2, GROUP), spec(1, 2, GROUP)],
            out_specs=[out_spec] * 3,
        ),
        out_shape=[out_shape] * 3,
        name="temporal_finish",
    )(place, mine, swapped, back, back_other)


def local(
    space_query, space_key, space_value, space_grad, time_query, time_key, time_value, time_grad
):
    def flat(array):
        return array.reshape(array.shape[1:])

    packed = pack_heads(*map(flat, (space_query, space_key, space_value, space_grad)))
    packed = lax.all_to_all(packed, "space", 0, 0, tiled=True)
    pieces = temporal_grads(*map(flat, (time_query, time_key, time_value, time_grad)))
    packed, pieces = lax.optimization_barrier((packed, pieces))
    packed = lax.all_to_all(spatial_grads(packed), "space", 0, 0, tiled=True)
    outs = tuple(unpack_heads(packed)) + tuple(temporal_finish(*pieces))
    return tuple(out.reshape(space_query.shape) for out in outs)


def solution(mesh):
    spec = P(None, "tm", "space", None)
    return jax.shard_map(
        local, mesh=mesh, in_specs=(spec,) * 8, out_specs=(spec,) * 6, check_vma=False
    )
```

```python
import functools
import math

import jax
import jax.numpy as jnp
from jax import lax
from jax.experimental import pallas as pl
from jax.experimental.pallas import tpu as pltpu
from jax.sharding import PartitionSpec as P

HEAD_DIM = 128
SCALE = 1.0 / math.sqrt(HEAD_DIM)
LOG2E = 1.0 / math.log(2.0)


def cost(micros):
    return pl.CostEstimate(flops=int(micros * 1e9), bytes_accessed=0, transcendentals=0)


def dot(a, b, contract):
    return lax.dot_general(a, b, (contract, ((), ())), preferred_element_type=jnp.float32)


def pack_kernel(*refs):
    *ins, out = refs
    heads = out.shape[0]
    for a, ref in enumerate(ins):
        for h in range(heads):
            out[h, 0, a] = ref[0, :, h * HEAD_DIM : (h + 1) * HEAD_DIM]


def pack_heads(*arrays):
    frames, positions, width = arrays[0].shape
    heads = width // HEAD_DIM
    count = len(arrays)
    return pl.pallas_call(
        pack_kernel,
        grid=(frames,),
        in_specs=[pl.BlockSpec((1, positions, width), lambda f: (f, 0, 0))] * count,
        out_specs=pl.BlockSpec(
            (heads, 1, count, positions, HEAD_DIM), lambda f: (0, f, 0, 0, 0)
        ),
        out_shape=jax.ShapeDtypeStruct(
            (heads, frames, count, positions, HEAD_DIM), arrays[0].dtype
        ),
        cost_estimate=cost(5),
        name="pack_heads",
    )(*arrays)


def unpack_kernel(ref, *outs):
    heads = ref.shape[0]
    for a, out in enumerate(outs):
        for h in range(heads):
            out[0, :, h * HEAD_DIM : (h + 1) * HEAD_DIM] = ref[h, 0, a]


def unpack_heads(array):
    heads, frames, count, positions, _ = array.shape
    width = heads * HEAD_DIM
    return pl.pallas_call(
        unpack_kernel,
        grid=(frames,),
        in_specs=[
            pl.BlockSpec((heads, 1, count, positions, HEAD_DIM), lambda f: (0, f, 0, 0, 0))
        ],
        out_specs=[pl.BlockSpec((1, positions, width), lambda f: (f, 0, 0))] * count,
        out_shape=[jax.ShapeDtypeStruct((frames, positions, width), array.dtype)] * count,
        cost_estimate=cost(4),
        name="unpack_heads",
    )(array)


def spatial_kernel(block, ref, out):
    parts, _, _, rows, _ = ref.shape
    total = parts * rows
    query, key, value, grad = (ref[:, 0, a].reshape(total, HEAD_DIM) for a in range(4))
    key_t = key.T
    dkey = dvalue = None
    for start in range(0, total, block):
        q = query[start : start + block]
        g = grad[start : start + block]
        scores = dot(key, q, ((1,), (1,)))
        peak = jnp.max(scores, axis=0, keepdims=True)
        e = jnp.exp2((scores - peak) * (SCALE * LOG2E))
        pgrad = dot(value, g, ((1,), (1,)))
        probs = e * (1.0 / jnp.sum(e, axis=0, keepdims=True))
        weights = probs.astype(jnp.bfloat16)
        term = probs * pgrad
        delta = jnp.sum(term, axis=0, keepdims=True)
        sgrad = (term - probs * delta).astype(jnp.bfloat16)
        dq = dot(key_t, sgrad, ((1,), (0,))).T * SCALE
        out[start // rows : (start + block) // rows, 0, 0] = dq.astype(out.dtype).reshape(
            block // rows, rows, HEAD_DIM
        )
        dk = dot(sgrad, q, ((1,), (0,)))
        dv = dot(weights, g, ((1,), (0,)))
        dkey = dk if dkey is None else dkey + dk
        dvalue = dv if dvalue is None else dvalue + dv
    out[:, 0, 1] = (dkey * SCALE).astype(out.dtype).reshape(parts, rows, HEAD_DIM)
    out[:, 0, 2] = dvalue.astype(out.dtype).reshape(parts, rows, HEAD_DIM)


def spatial_grads(array):
    parts, frames, _, rows, _ = array.shape
    return pl.pallas_call(
        functools.partial(spatial_kernel, min(256, parts * rows)),
        grid=(frames,),
        in_specs=[pl.BlockSpec((parts, 1, 4, rows, HEAD_DIM), lambda f: (0, f, 0, 0, 0))],
        out_specs=pl.BlockSpec((parts, 1, 3, rows, HEAD_DIM), lambda f: (0, f, 0, 0, 0)),
        out_shape=jax.ShapeDtypeStruct((parts, frames, 3, rows, HEAD_DIM), array.dtype),
        compiler_params=pltpu.CompilerParams(vmem_limit_bytes=48 * 1024 * 1024),
        cost_estimate=cost(20),
        name="spatial_grads",
    )(array)


GROUP = 16
CHIPS = [(t, t ^ 2) for t in range(4)]
CORES = [(t, t ^ 1) for t in range(4)]
NEVER = -1e30


def ship_kernel(query, key, value, grad, same, other, sems):
    member = lax.axis_index("tm")
    chip, core = member // 2, member % 2
    width = same.shape[-1]

    def copy_all(first, second, row):
        copies = []
        for half, out in ((core, same), (1 - core, other)):
            columns = pl.ds(pl.multiple_of(half * width, width), width)
            for a, ref in enumerate((first, second)):
                copies.append(
                    pltpu.make_async_copy(
                        ref.at[:, pl.ds(row, GROUP), columns], out.at[a], sems.at[len(copies)]
                    )
                )
        for copy in copies:
            copy.start()
        for copy in copies:
            copy.wait()

    @pl.when(chip == 0)
    def _():
        copy_all(key, value, 0)

    @pl.when(chip == 1)
    def _():
        copy_all(query, grad, GROUP)


def ship_pack(query, key, value, grad):
    frames, _, width = query.shape
    shape = jax.ShapeDtypeStruct((2, frames, GROUP, width // 2), query.dtype)
    return pl.pallas_call(
        ship_kernel,
        in_specs=[pl.BlockSpec(memory_space=pl.ANY)] * 4,
        out_specs=[pl.BlockSpec(memory_space=pltpu.VMEM)] * 2,
        out_shape=[shape, shape],
        scratch_shapes=[pltpu.SemaphoreType.DMA((4,))],
        cost_estimate=cost(2),
        name="ship_pack",
    )(query, key, value, grad)


def swap_kernel(*refs):
    *ins, out, sems = refs
    core = lax.axis_index("tm") % 2
    width = out.shape[-1]
    columns = pl.ds(pl.multiple_of((1 - core) * width, width), width)
    copies = [
        pltpu.make_async_copy(ref.at[:, :, columns], out.at[a], sems.at[a])
        for a, ref in enumerate(ins)
    ]
    for copy in copies:
        copy.start()
    for copy in copies:
        copy.wait()


def swap_pack(*arrays):
    frames, positions, width = arrays[0].shape
    count = len(arrays)
    return pl.pallas_call(
        swap_kernel,
        in_specs=[pl.BlockSpec(memory_space=pl.ANY)] * count,
        out_specs=pl.BlockSpec(memory_space=pltpu.VMEM),
        out_shape=jax.ShapeDtypeStruct((count, frames, positions, width // 2), arrays[0].dtype),
        scratch_shapes=[pltpu.SemaphoreType.DMA((count,))],
        cost_estimate=cost(3),
        name="swap_pack",
    )(*arrays)


def frame_mask(core, chip_frames, causal):
    rows = chip_frames * GROUP
    half = chip_frames // 2
    key_row = lax.broadcasted_iota(jnp.int32, (rows, rows), 0)
    query_row = lax.broadcasted_iota(jnp.int32, (rows, rows), 1)
    same = key_row % GROUP == query_row % GROUP
    key_frame = (key_row // GROUP + core * half) % chip_frames
    query_frame = (query_row // GROUP + core * half) % chip_frames
    return same & ((key_frame <= query_frame) | jnp.logical_not(causal))


def gather_rows(own, other, row, columns):
    rows = pl.ds(row, GROUP)
    return jnp.concatenate(
        [
            own[:, rows, columns].reshape(-1, HEAD_DIM),
            other[:, rows, columns].reshape(-1, HEAD_DIM),
        ],
        axis=0,
    )


def block_stats(mask, query, key, value, grad):
    scores = dot(key, query, ((1,), (1,))) * (SCALE * LOG2E)
    scores = jnp.where(mask, scores, NEVER)
    peak = jnp.max(scores, axis=0, keepdims=True)
    e = jnp.exp2(scores - peak)
    pgrad = dot(value, grad, ((1,), (1,)))
    return (
        (scores, pgrad),
        (peak, jnp.sum(e, axis=0, keepdims=True), jnp.sum(e * pgrad, axis=0, keepdims=True)),
    )


def block_grads(products, stats, more, query, key, grad):
    scores, pgrad = products
    peak = jnp.maximum(stats[0], more[0])
    own_scale, more_scale = jnp.exp2(stats[0] - peak), jnp.exp2(more[0] - peak)
    inverse = 1.0 / (stats[1] * own_scale + more[1] * more_scale)
    delta = (stats[2] * own_scale + more[2] * more_scale) * inverse
    probs = jnp.exp2(scores - peak) * inverse
    weights = probs.astype(jnp.bfloat16)
    sgrad = (probs * (pgrad - delta)).astype(jnp.bfloat16)
    dquery = dot(sgrad, key, ((0,), (0,))) * SCALE
    dkey = dot(sgrad, query, ((1,), (0,))) * SCALE
    dvalue = dot(weights, grad, ((1,), (0,)))
    return dquery, dkey, dvalue


def stats_kernel(place, query, key, value, grad, swapped, out):
    mask = frame_mask(place[0], 2 * query.shape[0], True)
    for h in range(query.shape[-1] // HEAD_DIM):
        columns = pl.ds(h * HEAD_DIM, HEAD_DIM)
        rows = [
            gather_rows(ref, swapped.at[a], 0, columns)
            for a, ref in enumerate((query, key, value, grad))
        ]
        out[h] = stats_rows(block_stats(mask, *rows)[1])


def stats_rows(stats):
    return jnp.concatenate(stats + (jnp.zeros((5, stats[0].shape[1]), jnp.float32),), axis=0)


def choose(first, when_first, when_second):
    return tuple(jnp.where(first, a, b) for a, b in zip(when_first, when_second))


def no_stats(rows):
    zero = jnp.zeros((1, rows), jnp.float32)
    return (zero + NEVER, zero, zero)


def place_rows(own, others, a, columns, values):
    values = values.astype(jnp.bfloat16).reshape(2, -1, GROUP, HEAD_DIM)
    own[a, :, :, columns] = values[0]
    others[a, :, :, columns] = values[1]


def early_kernel(
    place, query, key, value, grad, swapped, late_key, late_value, late_swapped, same, other, far,
    early, early_other, near, near_other, back, back_other, stats_out,
):
    core, first = place[0], place[1] == 0
    frames = query.shape[0]
    causal = frame_mask(core, 2 * frames, True)
    cross = frame_mask(core, 2 * frames, False)
    for h in range(query.shape[-1] // HEAD_DIM):
        columns = pl.ds(h * HEAD_DIM, HEAD_DIM)
        rows = [
            gather_rows(ref, swapped.at[a], 0, columns)
            for a, ref in enumerate((query, key, value, grad))
        ]
        late = [
            gather_rows(ref, late_swapped.at[a], 0, columns)
            for a, ref in ((1, late_key), (2, late_value))
        ]
        sent = [gather_rows(same.at[a], other.at[a], 0, columns) for a in range(2)]
        crossed = [
            jnp.where(first, sent[0], rows[0]),
            jnp.where(first, late[0], sent[0]),
            jnp.where(first, late[1], sent[1]),
            jnp.where(first, sent[1], rows[3]),
        ]
        received = tuple(far[h, i : i + 1] for i in range(3))
        products, stats = block_stats(causal, *rows)
        cross_products, cross_stats = block_stats(cross, *crossed)
        stats_out[h] = stats_rows(cross_stats)
        none = no_stats(2 * frames * GROUP)
        out = block_grads(
            products, stats, choose(first, none, cross_stats), rows[0], rows[1], rows[3]
        )
        cross_out = block_grads(
            cross_products,
            cross_stats,
            choose(first, received, stats),
            crossed[0],
            crossed[1],
            crossed[3],
        )
        zero = jnp.zeros_like(cross_out[0])
        place_rows(early, early_other, 0, columns, out[0] + jnp.where(first, zero, cross_out[0]))
        place_rows(early, early_other, 1, columns, out[1])
        place_rows(early, early_other, 2, columns, out[2])
        place_rows(near, near_other, 0, columns, cross_out[1])
        place_rows(near, near_other, 1, columns, cross_out[2])
        place_rows(
            back, back_other, 0, columns, jnp.where(first, cross_out[0], cross_out[1])
        )
        place_rows(back, back_other, 1, columns, jnp.where(first, zero, cross_out[2]))


def late_kernel(
    place, query, key, value, grad, swapped, far, early, early_other, near, near_other, back,
    back_other, dquery, dkey, dvalue, theirs,
):
    core, first = place[0], place[1] == 0
    frames = query.shape[0]
    causal = frame_mask(core, 2 * frames, True)
    early_rows, late_rows = pl.ds(0, GROUP), pl.ds(GROUP, GROUP)
    for h in range(query.shape[-1] // HEAD_DIM):
        columns = pl.ds(h * HEAD_DIM, HEAD_DIM)
        rows = [
            gather_rows(ref, swapped.at[a], 0, columns)
            for a, ref in enumerate((query, key, value, grad))
        ]
        received = tuple(far[h, i : i + 1] for i in range(3))
        products, stats = block_stats(causal, *rows)
        none = no_stats(2 * frames * GROUP)
        late = [
            values.reshape(2, frames, GROUP, HEAD_DIM)
            for values in block_grads(
                products, stats, choose(first, none, received), rows[0], rows[1], rows[3]
            )
        ]

        def write(outs, side, near, back, early):
            zero = jnp.zeros((frames, GROUP, HEAD_DIM), jnp.float32)
            back = [back[a, :, :, columns].astype(jnp.float32) for a in range(2)]
            near = [near[a, :, :, columns].astype(jnp.float32) for a in range(2)]
            early = [early[a, :, :, columns].astype(jnp.float32) for a in range(3)]
            early[1] += jnp.where(first, back[0], zero)
            early[2] += jnp.where(first, back[1], zero)
            more = (
                jnp.where(first, zero, back[0]),
                jnp.where(first, near[0], zero),
                jnp.where(first, near[1], zero),
            )
            for a, out in enumerate(outs):
                out[:, early_rows, columns] = early[a].astype(jnp.bfloat16)
                out[:, late_rows, columns] = (late[a][side] + more[a]).astype(jnp.bfloat16)

        write((dquery, dkey, dvalue), 0, near, back, early)
        write([theirs.at[a] for a in range(3)], 1, near_other, back_other, early_other)


def finish_kernel(place, swapped, *refs):
    for a, out in enumerate(refs[3:]):
        out[...] = swapped[a]


STEPS = 4


class Temporal:
    def __init__(self, arrays):
        self.arrays = arrays
        self.frames, self.positions, self.width = arrays[0].shape
        self.half = self.width // 2
        self.block = self.half // STEPS
        self.heads = self.half // HEAD_DIM
        member = lax.axis_index("tm")
        self.place = jnp.stack([member % 2, member // 2])

    def own(self, row):
        return pl.BlockSpec(
            (self.frames, GROUP, self.block), lambda j, p: (0, row, p[0] * STEPS + j)
        )

    def part(self, count, rows, row=0):
        return pl.BlockSpec((count, self.frames, rows, self.block), lambda j, p: (0, 0, row, j))

    def stats(self):
        return pl.BlockSpec(
            (self.heads // STEPS, 8, 2 * self.frames * GROUP), lambda j, p: (j, 0, 0)
        )

    def stats_shape(self):
        return jax.ShapeDtypeStruct((self.heads, 8, 2 * self.frames * GROUP), jnp.float32)

    def shape(self, count, rows):
        return jax.ShapeDtypeStruct((count, self.frames, rows, self.half), jnp.bfloat16)

    def call(self, kernel, name, micros, in_specs, out_specs, out_shape, operands, aliases={}):
        return pl.pallas_call(
            kernel,
            grid_spec=pltpu.PrefetchScalarGridSpec(
                num_scalar_prefetch=1, grid=(STEPS,), in_specs=in_specs, out_specs=out_specs
            ),
            out_shape=out_shape,
            input_output_aliases=aliases,
            cost_estimate=cost(micros),
            name=name,
        )(self.place, *operands)

    def late_stats(self, swapped):
        return self.call(
            stats_kernel,
            "temporal_stats",
            5,
            [self.own(1)] * 4 + [self.part(4, GROUP, 1)],
            self.stats(),
            self.stats_shape(),
            self.arrays + (swapped,),
        )

    def early_grads(self, swapped, same, other, far):
        return self.call(
            early_kernel,
            "temporal_early",
            EARLY_COST,
            [self.own(0)] * 4
            + [self.part(4, GROUP)]
            + [self.own(1)] * 2
            + [self.part(4, GROUP, 1)]
            + [self.part(2, GROUP)] * 2
            + [self.stats()],
            [self.part(3, GROUP)] * 2 + [self.part(2, GROUP)] * 4 + [self.stats()],
            [self.shape(3, GROUP)] * 2 + [self.shape(2, GROUP)] * 4 + [self.stats_shape()],
            self.arrays
            + (swapped, self.arrays[1], self.arrays[2], swapped, same, other, far),
        )

    def late_grads(self, swapped, far, *parts):
        out = pl.BlockSpec(
            (self.frames, self.positions, self.block), lambda j, p: (0, 0, p[0] * STEPS + j)
        )
        out_shape = jax.ShapeDtypeStruct((self.frames, self.positions, self.width), jnp.bfloat16)
        return self.call(
            late_kernel,
            "temporal_late",
            LATE_COST,
            [self.own(1)] * 4
            + [self.part(4, GROUP, 1), self.stats()]
            + [self.part(3, GROUP)] * 2
            + [self.part(2, GROUP)] * 4,
            [out] * 3 + [self.part(3, self.positions)],
            [out_shape] * 3 + [self.shape(3, self.positions)],
            self.arrays + (swapped, far) + parts,
        )

    def finish(self, outs, swapped):
        out = pl.BlockSpec(
            (self.frames, self.positions, self.block),
            lambda j, p: (0, 0, (1 - p[0]) * STEPS + j),
        )
        return self.call(
            finish_kernel,
            "temporal_finish",
            3,
            [self.part(3, self.positions)] + [pl.BlockSpec(memory_space=pl.ANY)] * 3,
            [out] * 3,
            [jax.ShapeDtypeStruct(a.shape, a.dtype) for a in outs],
            (swapped,) + tuple(outs),
            {2: 0, 3: 1, 4: 2},
        )


EARLY_COST = 100
LATE_COST = 100


def local(
    space_query, space_key, space_value, space_grad, time_query, time_key, time_value, time_grad
):
    def flat(array):
        return array.reshape(array.shape[1:])

    def chips(array):
        return lax.ppermute(array, "tm", CHIPS)

    def cores(array):
        return lax.ppermute(array, "tm", CORES)

    spatial = tuple(map(flat, (space_query, space_key, space_value, space_grad)))
    arrays = tuple(map(flat, (time_query, time_key, time_value, time_grad)))

    ships, arrays, spatial = lax.optimization_barrier((ship_pack(*arrays), arrays, spatial))
    same, other = map(chips, ships)
    swapped = cores(swap_pack(*arrays))
    work = Temporal(arrays)
    packed, far, other = lax.optimization_barrier(
        (pack_heads(*spatial), work.late_stats(swapped), other)
    )
    far = chips(far)
    packed = lax.all_to_all(packed, "space", 0, 0, tiled=True)
    early, early_other, near, near_other, back, back_other, far = work.early_grads(
        swapped, same, cores(other), far
    )
    far, back_other, back = chips(far), chips(back_other), chips(back)
    packed, far, back, back_other = lax.optimization_barrier(
        (spatial_grads(packed), far, back, back_other)
    )
    packed = lax.all_to_all(packed, "space", 0, 0, tiled=True)
    *outs, theirs = work.late_grads(
        swapped, far, early, early_other, near, near_other, back, back_other
    )
    outs = work.finish(outs, cores(theirs))
    outs = tuple(unpack_heads(packed)) + tuple(outs)
    return tuple(out.reshape(space_query.shape) for out in outs)


def solution(mesh):
    spec = P(None, "tm", "space", None)
    return jax.shard_map(
        local, mesh=mesh, in_specs=(spec,) * 8, out_specs=(spec,) * 6, check_vma=False
    )
```

```python
import functools
import math

import jax
import jax.numpy as jnp
from jax import lax
from jax.experimental import pallas as pl
from jax.experimental.pallas import tpu as pltpu
from jax.sharding import PartitionSpec as P

HEAD_DIM = 128
SCALE = 1.0 / math.sqrt(HEAD_DIM)
LOG2E = 1.0 / math.log(2.0)
MIB = 1024 * 1024
PARAMS = pltpu.CompilerParams(vmem_limit_bytes=60 * MIB)
LATE_PARAMS = pltpu.CompilerParams(vmem_limit_bytes=59 * MIB)
UNPACK_PARAMS = pltpu.CompilerParams(vmem_limit_bytes=16 * MIB)


def cost(micros):
    return pl.CostEstimate(flops=int(micros * 1e9), bytes_accessed=0, transcendentals=0)


def dot(a, b, contract):
    return lax.dot_general(a, b, (contract, ((), ())), preferred_element_type=jnp.float32)


def pack_kernel(*refs):
    *ins, out, rows, heads, row_sems, head_sems = refs
    count, frames = rows.shape[:2]

    def load(f, a):
        return pltpu.make_async_copy(ins[a].at[f], rows.at[a, f], row_sems.at[f, a])

    def store(f):
        return pltpu.make_async_copy(heads.at[:, f], out.at[:, f], head_sems.at[f])

    for f in range(frames):
        for a in range(count):
            load(f, a).start()
    for f in range(frames):
        for a in range(count):
            load(f, a).wait()
            for h in range(heads.shape[0]):
                heads[h, f, a] = rows[a, f, :, h * HEAD_DIM : (h + 1) * HEAD_DIM]
        store(f).start()
    for f in range(frames):
        store(f).wait()


def pack_heads(*arrays):
    frames, positions, width = arrays[0].shape
    count, heads = len(arrays), width // HEAD_DIM
    dtype = arrays[0].dtype
    packed = (heads, frames, count, positions, HEAD_DIM)
    return pl.pallas_call(
        pack_kernel,
        in_specs=[pl.BlockSpec(memory_space=pltpu.HBM)] * count,
        out_specs=pl.BlockSpec(memory_space=pl.ANY),
        out_shape=jax.ShapeDtypeStruct(packed, dtype),
        scratch_shapes=[
            pltpu.VMEM((count, frames, positions, width), dtype),
            pltpu.VMEM(packed, dtype),
            pltpu.SemaphoreType.DMA((frames, count)),
            pltpu.SemaphoreType.DMA((frames,)),
        ],
        compiler_params=PARAMS,
        cost_estimate=cost(5),
        name="pack_heads",
    )(*arrays)


def unpack_kernel(ref, *outs):
    heads = ref.shape[0]
    for a, out in enumerate(outs):
        for h in range(heads):
            out[0, :, h * HEAD_DIM : (h + 1) * HEAD_DIM] = ref[h, 0, a]


def unpack_heads(array):
    heads, frames, count, positions, _ = array.shape
    width = heads * HEAD_DIM
    return pl.pallas_call(
        unpack_kernel,
        grid=(frames,),
        in_specs=[
            pl.BlockSpec((heads, 1, count, positions, HEAD_DIM), lambda f: (0, f, 0, 0, 0))
        ],
        out_specs=[pl.BlockSpec((1, positions, width), lambda f: (f, 0, 0))] * count,
        out_shape=[jax.ShapeDtypeStruct((frames, positions, width), array.dtype)] * count,
        compiler_params=UNPACK_PARAMS,
        cost_estimate=cost(4),
        name="unpack_heads",
    )(array)


def spatial_kernel(block, ref, out):
    parts, _, _, rows, _ = ref.shape
    total = parts * rows
    query, key, value, grad = (ref[:, 0, a].reshape(total, HEAD_DIM) for a in range(4))
    key_t = key.T
    dkey = dvalue = None
    for start in range(0, total, block):
        q = query[start : start + block]
        g = grad[start : start + block]
        scores = dot(key, q, ((1,), (1,)))
        peak = jnp.max(scores, axis=0, keepdims=True)
        e = jnp.exp2((scores - peak) * (SCALE * LOG2E))
        pgrad = dot(value, g, ((1,), (1,)))
        probs = e * (1.0 / jnp.sum(e, axis=0, keepdims=True))
        weights = probs.astype(jnp.bfloat16)
        term = probs * pgrad
        delta = jnp.sum(term, axis=0, keepdims=True)
        sgrad = (term - probs * delta).astype(jnp.bfloat16)
        dq = dot(key_t, sgrad, ((1,), (0,))).T * SCALE
        out[start // rows : (start + block) // rows, 0, 0] = dq.astype(out.dtype).reshape(
            block // rows, rows, HEAD_DIM
        )
        dk = dot(sgrad, q, ((1,), (0,)))
        dv = dot(weights, g, ((1,), (0,)))
        dkey = dk if dkey is None else dkey + dk
        dvalue = dv if dvalue is None else dvalue + dv
    out[:, 0, 1] = (dkey * SCALE).astype(out.dtype).reshape(parts, rows, HEAD_DIM)
    out[:, 0, 2] = dvalue.astype(out.dtype).reshape(parts, rows, HEAD_DIM)


def spatial_grads(array):
    parts, frames, _, rows, _ = array.shape
    return pl.pallas_call(
        functools.partial(spatial_kernel, min(1024, parts * rows)),
        grid=(frames,),
        in_specs=[pl.BlockSpec((parts, 1, 4, rows, HEAD_DIM), lambda f: (0, f, 0, 0, 0))],
        out_specs=pl.BlockSpec((parts, 1, 3, rows, HEAD_DIM), lambda f: (0, f, 0, 0, 0)),
        out_shape=jax.ShapeDtypeStruct((parts, frames, 3, rows, HEAD_DIM), array.dtype),
        compiler_params=PARAMS,
        cost_estimate=cost(20),
        name="spatial_grads",
    )(array)


GROUP = 16
CHIPS = [(t, t ^ 2) for t in range(4)]
CORES = [(t, t ^ 1) for t in range(4)]
CROSSED = [(t, t ^ 3) for t in range(4)]
NEVER = -1e30


def ship_kernel(query, key, value, grad, same, other, swap, sems):
    member = lax.axis_index("tm")
    chip, core = member // 2, member % 2
    width = same.shape[-1]
    own_columns = pl.ds(pl.multiple_of(core * width, width), width)
    other_columns = pl.ds(pl.multiple_of((1 - core) * width, width), width)

    def copy_all(first, second, row):
        rows = pl.ds(row, GROUP)
        pairs = [
            (ref.at[:, rows, columns], out.at[a])
            for columns, out in ((other_columns, other), (own_columns, same))
            for a, ref in enumerate((first, second))
        ]
        pairs += [
            (ref.at[:, :, other_columns], swap.at[a])
            for a, ref in enumerate((query, key, value, grad))
        ]
        copies = [
            pltpu.make_async_copy(source, target, sems.at[i])
            for i, (source, target) in enumerate(pairs)
        ]
        for copy in copies:
            copy.start()
        for copy in copies:
            copy.wait()

    @pl.when(chip == 0)
    def _():
        copy_all(key, value, 0)

    @pl.when(chip == 1)
    def _():
        copy_all(query, grad, GROUP)


def ship_pack(query, key, value, grad):
    frames, positions, width = query.shape
    half = width // 2
    shape = jax.ShapeDtypeStruct((2, frames, GROUP, half), query.dtype)
    swap_shape = jax.ShapeDtypeStruct((4, frames, positions, half), query.dtype)
    return pl.pallas_call(
        ship_kernel,
        in_specs=[pl.BlockSpec(memory_space=pltpu.HBM)] * 4,
        out_specs=[pl.BlockSpec(memory_space=pltpu.VMEM)] * 3,
        out_shape=[shape, shape, swap_shape],
        scratch_shapes=[pltpu.SemaphoreType.DMA((8,))],
        compiler_params=PARAMS,
        cost_estimate=cost(2),
        name="ship_pack",
    )(query, key, value, grad)


def frame_mask(core, chip_frames, causal):
    rows = chip_frames * GROUP
    half = chip_frames // 2
    key_row = lax.broadcasted_iota(jnp.int32, (rows, rows), 0)
    query_row = lax.broadcasted_iota(jnp.int32, (rows, rows), 1)
    same = key_row % GROUP == query_row % GROUP
    key_frame = (key_row // GROUP + core * half) % chip_frames
    query_frame = (query_row // GROUP + core * half) % chip_frames
    return same & ((key_frame <= query_frame) | jnp.logical_not(causal))


def gather_rows(own, other, row, columns):
    rows = pl.ds(row, GROUP)
    return jnp.concatenate(
        [
            own[:, rows, columns].reshape(-1, HEAD_DIM),
            other[:, rows, columns].reshape(-1, HEAD_DIM),
        ],
        axis=0,
    )


def block_stats(mask, query, key, value, grad):
    scores = dot(key, query, ((1,), (1,))) * (SCALE * LOG2E)
    scores = jnp.where(mask, scores, NEVER)
    peak = jnp.max(scores, axis=0, keepdims=True)
    e = jnp.exp2(scores - peak)
    pgrad = dot(value, grad, ((1,), (1,)))
    return (
        (scores, pgrad),
        (peak, jnp.sum(e, axis=0, keepdims=True), jnp.sum(e * pgrad, axis=0, keepdims=True)),
    )


def block_grads(products, stats, more, query, key, grad):
    scores, pgrad = products
    peak = jnp.maximum(stats[0], more[0])
    own_scale, more_scale = jnp.exp2(stats[0] - peak), jnp.exp2(more[0] - peak)
    inverse = 1.0 / (stats[1] * own_scale + more[1] * more_scale)
    delta = (stats[2] * own_scale + more[2] * more_scale) * inverse
    probs = jnp.exp2(scores - peak) * inverse
    weights = probs.astype(jnp.bfloat16)
    sgrad = (probs * (pgrad - delta)).astype(jnp.bfloat16)
    dquery = dot(sgrad, key, ((0,), (0,))) * SCALE
    dkey = dot(sgrad, query, ((1,), (0,))) * SCALE
    dvalue = dot(weights, grad, ((1,), (0,)))
    return dquery, dkey, dvalue


def stats_kernel(place, query, key, value, grad, swapped, out):
    mask = frame_mask(place[0] % 2, 2 * query.shape[0], True)
    for h in range(query.shape[-1] // HEAD_DIM):
        columns = pl.ds(h * HEAD_DIM, HEAD_DIM)
        rows = [
            gather_rows(ref, swapped.at[a], 0, columns)
            for a, ref in enumerate((query, key, value, grad))
        ]
        out[h] = stats_rows(block_stats(mask, *rows)[1])


def stats_rows(stats):
    return jnp.concatenate(stats + (jnp.zeros((5, stats[0].shape[1]), jnp.float32),), axis=0)


def choose(first, when_first, when_second):
    return tuple(jnp.where(first, a, b) for a, b in zip(when_first, when_second))


def no_stats(rows):
    zero = jnp.zeros((1, rows), jnp.float32)
    return (zero + NEVER, zero, zero)


def place_rows(own, others, a, columns, values):
    values = values.astype(jnp.bfloat16).reshape(2, -1, GROUP, HEAD_DIM)
    own[a, :, :, columns] = values[0]
    others[a, :, :, columns] = values[1]


def early_kernel(
    place, query, key, value, grad, swapped, late_key, late_value, late_swapped, same, other, far,
    early, early_other, near, near_other, back, back_other, stats_out,
):
    core, first = place[0] % 2, place[0] < 2
    frames = query.shape[0]
    causal = frame_mask(core, 2 * frames, True)
    cross = frame_mask(core, 2 * frames, False)
    for h in range(query.shape[-1] // HEAD_DIM):
        columns = pl.ds(h * HEAD_DIM, HEAD_DIM)
        rows = [
            gather_rows(ref, swapped.at[a], 0, columns)
            for a, ref in enumerate((query, key, value, grad))
        ]
        late = [
            gather_rows(ref, late_swapped.at[a], 0, columns)
            for a, ref in ((1, late_key), (2, late_value))
        ]
        sent = [gather_rows(same.at[a], other.at[a], 0, columns) for a in range(2)]
        crossed = [
            jnp.where(first, sent[0], rows[0]),
            jnp.where(first, late[0], sent[0]),
            jnp.where(first, late[1], sent[1]),
            jnp.where(first, sent[1], rows[3]),
        ]
        received = tuple(far[h, i : i + 1] for i in range(3))
        products, stats = block_stats(causal, *rows)
        cross_products, cross_stats = block_stats(cross, *crossed)
        stats_out[h] = stats_rows(cross_stats)
        none = no_stats(2 * frames * GROUP)
        out = block_grads(
            products, stats, choose(first, none, cross_stats), rows[0], rows[1], rows[3]
        )
        cross_out = block_grads(
            cross_products,
            cross_stats,
            choose(first, received, stats),
            crossed[0],
            crossed[1],
            crossed[3],
        )
        zero = jnp.zeros_like(cross_out[0])
        place_rows(early, early_other, 0, columns, out[0] + jnp.where(first, zero, cross_out[0]))
        place_rows(early, early_other, 1, columns, out[1])
        place_rows(early, early_other, 2, columns, out[2])
        place_rows(near, near_other, 0, columns, cross_out[1])
        place_rows(near, near_other, 1, columns, cross_out[2])
        place_rows(
            back, back_other, 0, columns, jnp.where(first, cross_out[0], cross_out[1])
        )
        place_rows(back, back_other, 1, columns, jnp.where(first, zero, cross_out[2]))


def late_kernel(
    place, query, key, value, grad, swapped, far, early, early_other, near, near_other, back,
    back_other, dquery, dkey, dvalue, theirs,
):
    core, first = place[0] % 2, place[0] < 2
    frames = query.shape[0]
    causal = frame_mask(core, 2 * frames, True)
    early_rows, late_rows = pl.ds(0, GROUP), pl.ds(GROUP, GROUP)
    for h in range(query.shape[-1] // HEAD_DIM):
        columns = pl.ds(h * HEAD_DIM, HEAD_DIM)
        rows = [
            gather_rows(ref, swapped.at[a], 0, columns)
            for a, ref in enumerate((query, key, value, grad))
        ]
        received = tuple(far[h, i : i + 1] for i in range(3))
        products, stats = block_stats(causal, *rows)
        none = no_stats(2 * frames * GROUP)
        late = [
            values.reshape(2, frames, GROUP, HEAD_DIM)
            for values in block_grads(
                products, stats, choose(first, none, received), rows[0], rows[1], rows[3]
            )
        ]

        def write(outs, side, near, back, early):
            zero = jnp.zeros((frames, GROUP, HEAD_DIM), jnp.float32)
            back = [back[a, :, :, columns].astype(jnp.float32) for a in range(2)]
            near = [near[a, :, :, columns].astype(jnp.float32) for a in range(2)]
            early = [early[a, :, :, columns].astype(jnp.float32) for a in range(3)]
            early[1] += jnp.where(first, back[0], zero)
            early[2] += jnp.where(first, back[1], zero)
            more = (
                jnp.where(first, zero, back[0]),
                jnp.where(first, near[0], zero),
                jnp.where(first, near[1], zero),
            )
            for a, out in enumerate(outs):
                out[:, early_rows, columns] = early[a].astype(jnp.bfloat16)
                out[:, late_rows, columns] = (late[a][side] + more[a]).astype(jnp.bfloat16)

        write((dquery, dkey, dvalue), 0, near, back, early)
        write([theirs.at[a] for a in range(3)], 1, near_other, back_other, early_other)


def finish_kernel(place, swapped, *refs):
    for a, out in enumerate(refs[3:]):
        out[...] = swapped[a]


STATS_STEPS, EARLY_STEPS, LATE_STEPS, FINISH_STEPS = 2, 4, 4, 4


class Temporal:
    def __init__(self, arrays):
        self.arrays = arrays
        self.frames, self.positions, self.width = arrays[0].shape
        self.half = self.width // 2
        self.heads = self.half // HEAD_DIM
        member = lax.axis_index("tm")
        self.place = member.reshape(1)

    def own(self, steps, row):
        return pl.BlockSpec(
            (self.frames, GROUP, self.half // steps),
            lambda j, p: (0, row, (p[0] % 2) * steps + j),
        )

    def part(self, steps, count, rows, row=0):
        return pl.BlockSpec(
            (count, self.frames, rows, self.half // steps), lambda j, p: (0, 0, row, j)
        )

    def stats(self, steps):
        return pl.BlockSpec(
            (self.heads // steps, 8, 2 * self.frames * GROUP), lambda j, p: (j, 0, 0)
        )

    def stats_shape(self):
        return jax.ShapeDtypeStruct((self.heads, 8, 2 * self.frames * GROUP), jnp.float32)

    def shape(self, count, rows):
        return jax.ShapeDtypeStruct((count, self.frames, rows, self.half), jnp.bfloat16)

    def call(self, steps, kernel, name, micros, in_specs, out_specs, out_shape, operands, params=PARAMS, aliases={}):
        return pl.pallas_call(
            kernel,
            grid_spec=pltpu.PrefetchScalarGridSpec(
                num_scalar_prefetch=1, grid=(steps,), in_specs=in_specs, out_specs=out_specs
            ),
            out_shape=out_shape,
            input_output_aliases=aliases,
            compiler_params=PARAMS,
        cost_estimate=cost(micros),
            name=name,
        )(self.place, *operands)

    def late_stats(self, swapped):
        return self.call(
            STATS_STEPS,
            stats_kernel,
            "temporal_stats",
            5,
            [self.own(STATS_STEPS, 1)] * 4 + [self.part(STATS_STEPS, 4, GROUP, 1)],
            self.stats(STATS_STEPS),
            self.stats_shape(),
            self.arrays + (swapped,),
        )

    def early_grads(self, swapped, same, other, far):
        return self.call(
            EARLY_STEPS,
            early_kernel,
            "temporal_early",
            EARLY_COST,
            [self.own(EARLY_STEPS, 0)] * 4
            + [self.part(EARLY_STEPS, 4, GROUP)]
            + [self.own(EARLY_STEPS, 1)] * 2
            + [self.part(EARLY_STEPS, 4, GROUP, 1)]
            + [self.part(EARLY_STEPS, 2, GROUP)] * 2
            + [self.stats(EARLY_STEPS)],
            [self.part(EARLY_STEPS, 3, GROUP)] * 2 + [self.part(EARLY_STEPS, 2, GROUP)] * 4 + [self.stats(EARLY_STEPS)],
            [self.shape(3, GROUP)] * 2 + [self.shape(2, GROUP)] * 4 + [self.stats_shape()],
            self.arrays
            + (swapped, self.arrays[1], self.arrays[2], swapped, same, other, far),
        )

    def late_grads(self, swapped, far, *parts):
        out = pl.BlockSpec(
            (self.frames, self.positions, self.half // LATE_STEPS), lambda j, p: (0, 0, (p[0] % 2) * LATE_STEPS + j)
        )
        out_shape = jax.ShapeDtypeStruct((self.frames, self.positions, self.width), jnp.bfloat16)
        return self.call(
            LATE_STEPS,
            late_kernel,
            "temporal_late",
            LATE_COST,
            [self.own(LATE_STEPS, 1)] * 4
            + [self.part(LATE_STEPS, 4, GROUP, 1), self.stats(LATE_STEPS)]
            + [self.part(LATE_STEPS, 3, GROUP)] * 2
            + [self.part(LATE_STEPS, 2, GROUP)] * 4,
            [out] * 3 + [self.part(LATE_STEPS, 3, self.positions)],
            [out_shape] * 3 + [self.shape(3, self.positions)],
            self.arrays + (swapped, far) + parts,
            LATE_PARAMS,
        )

    def finish(self, outs, swapped):
        out = pl.BlockSpec(
            (self.frames, self.positions, self.half // FINISH_STEPS),
            lambda j, p: (0, 0, (1 - p[0] % 2) * FINISH_STEPS + j),
        )
        return self.call(
            FINISH_STEPS,
            finish_kernel,
            "temporal_finish",
            3,
            [self.part(FINISH_STEPS, 3, self.positions)] + [pl.BlockSpec(memory_space=pl.ANY)] * 3,
            [out] * 3,
            [jax.ShapeDtypeStruct(a.shape, a.dtype) for a in outs],
            (swapped,) + tuple(outs),
            LATE_PARAMS,
            {2: 0, 3: 1, 4: 2},
        )


EARLY_COST = 100
LATE_COST = 100


def local(
    space_query, space_key, space_value, space_grad, time_query, time_key, time_value, time_grad
):
    def flat(array):
        return array.reshape(array.shape[1:])

    def chips(array):
        return lax.ppermute(array, "tm", CHIPS)

    def crossed(array):
        return lax.ppermute(array, "tm", CROSSED)

    def cores(array):
        return lax.ppermute(array, "tm", CORES)

    spatial = tuple(map(flat, (space_query, space_key, space_value, space_grad)))
    arrays = tuple(map(flat, (time_query, time_key, time_value, time_grad)))

    ships, arrays, spatial = lax.optimization_barrier((ship_pack(*arrays), arrays, spatial))
    same, other, swapped = chips(ships[0]), crossed(ships[1]), cores(ships[2])
    work = Temporal(arrays)
    packed, far = lax.optimization_barrier((pack_heads(*spatial), work.late_stats(swapped)))
    far = chips(far)
    packed = lax.all_to_all(packed, "space", 0, 0, tiled=True)
    early, early_other, near, near_other, back, back_other, far = work.early_grads(
        swapped, same, other, far
    )
    far, back_other, back = chips(far), chips(back_other), chips(back)
    packed = lax.all_to_all(spatial_grads(packed), "space", 0, 0, tiled=True)
    *outs, theirs = work.late_grads(
        swapped, far, early, early_other, near, near_other, back, back_other
    )
    outs = work.finish(outs, cores(theirs))
    outs = tuple(unpack_heads(packed)) + tuple(outs)
    return tuple(out.reshape(space_query.shape) for out in outs)


def solution(mesh):
    spec = P(None, "tm", "space", None)
    return jax.shard_map(
        local, mesh=mesh, in_specs=(spec,) * 8, out_specs=(spec,) * 6, check_vma=False
    )
```

```python
import math

import jax
import jax.numpy as jnp
from jax import lax
from jax.experimental import pallas as pl
from jax.experimental.pallas import tpu as pltpu
from jax.sharding import PartitionSpec as P

HEAD_DIM = 128
SCALE = 1.0 / math.sqrt(HEAD_DIM)
LOG2E = 1.0 / math.log(2.0)
MIB = 1024 * 1024
PARAMS = pltpu.CompilerParams(vmem_limit_bytes=60 * MIB)
LATE_PARAMS = pltpu.CompilerParams(vmem_limit_bytes=59 * MIB)
UNPACK_PARAMS = pltpu.CompilerParams(vmem_limit_bytes=16 * MIB)


def cost(micros):
    return pl.CostEstimate(flops=int(micros * 1e9), bytes_accessed=0, transcendentals=0)


def dot(a, b, contract):
    return lax.dot_general(a, b, (contract, ((), ())), preferred_element_type=jnp.float32)


def pack_kernel(*refs):
    *ins, out, rows, heads, row_sems, head_sems = refs
    count, frames = rows.shape[:2]

    def load(f, a):
        return pltpu.make_async_copy(ins[a].at[f], rows.at[a, f], row_sems.at[f, a])

    def store(f):
        return pltpu.make_async_copy(heads.at[:, f], out.at[:, f], head_sems.at[f])

    for f in range(frames):
        for a in range(count):
            load(f, a).start()
    for f in range(frames):
        for a in range(count):
            load(f, a).wait()
            for h in range(heads.shape[0]):
                heads[h, f, a] = rows[a, f, :, h * HEAD_DIM : (h + 1) * HEAD_DIM]
        store(f).start()
    for f in range(frames):
        store(f).wait()


def pack_heads(*arrays):
    frames, positions, width = arrays[0].shape
    count, heads = len(arrays), width // HEAD_DIM
    dtype = arrays[0].dtype
    packed = (heads, frames, count, positions, HEAD_DIM)
    return pl.pallas_call(
        pack_kernel,
        in_specs=[pl.BlockSpec(memory_space=pltpu.HBM)] * count,
        out_specs=pl.BlockSpec(memory_space=pl.ANY),
        out_shape=jax.ShapeDtypeStruct(packed, dtype),
        scratch_shapes=[
            pltpu.VMEM((count, frames, positions, width), dtype),
            pltpu.VMEM(packed, dtype),
            pltpu.SemaphoreType.DMA((frames, count)),
            pltpu.SemaphoreType.DMA((frames,)),
        ],
        compiler_params=PARAMS,
        cost_estimate=cost(5),
        name="pack_heads",
    )(*arrays)


def unpack_kernel(ref, *outs):
    heads = ref.shape[0]
    for a, out in enumerate(outs):
        for h in range(heads):
            out[0, :, h * HEAD_DIM : (h + 1) * HEAD_DIM] = ref[h, 0, a]


def unpack_heads(array):
    heads, frames, count, positions, _ = array.shape
    width = heads * HEAD_DIM
    return pl.pallas_call(
        unpack_kernel,
        grid=(frames,),
        in_specs=[
            pl.BlockSpec((heads, 1, count, positions, HEAD_DIM), lambda f: (0, f, 0, 0, 0))
        ],
        out_specs=[pl.BlockSpec((1, positions, width), lambda f: (f, 0, 0))] * count,
        out_shape=[jax.ShapeDtypeStruct((frames, positions, width), array.dtype)] * count,
        compiler_params=UNPACK_PARAMS,
        cost_estimate=cost(4),
        name="unpack_heads",
    )(array)


def spatial_kernel(ref, out):
    parts, _, _, rows, _ = ref.shape
    query, key, value, grad = (ref[:, 0, a].reshape(parts * rows, HEAD_DIM) for a in range(4))
    scores = dot(query, key, ((1,), (1,)))
    peak = jnp.max(scores, axis=1, keepdims=True)
    e = jnp.exp2((scores - peak) * (SCALE * LOG2E))
    pgrad = dot(grad, value, ((1,), (1,)))
    probs = e * (1.0 / jnp.sum(e, axis=1, keepdims=True))
    term = probs * pgrad
    delta = jnp.sum(term, axis=1, keepdims=True)
    sgrad = (term - probs * delta).astype(jnp.bfloat16)
    results = (
        dot(sgrad, key, ((1,), (0,))) * SCALE,
        dot(query.T, sgrad, ((1,), (0,))).T * SCALE,
        dot(grad.T, probs.astype(jnp.bfloat16), ((1,), (0,))).T,
    )
    for a, result in enumerate(results):
        out[:, 0, a] = result.astype(out.dtype).reshape(parts, rows, HEAD_DIM)


def spatial_grads(array):
    parts, frames, _, rows, _ = array.shape
    return pl.pallas_call(
        spatial_kernel,
        grid=(frames,),
        in_specs=[pl.BlockSpec((parts, 1, 4, rows, HEAD_DIM), lambda f: (0, f, 0, 0, 0))],
        out_specs=pl.BlockSpec((parts, 1, 3, rows, HEAD_DIM), lambda f: (0, f, 0, 0, 0)),
        out_shape=jax.ShapeDtypeStruct((parts, frames, 3, rows, HEAD_DIM), array.dtype),
        compiler_params=PARAMS,
        cost_estimate=cost(20),
        name="spatial_grads",
    )(array)


GROUP = 16
CHIPS = [(t, t ^ 2) for t in range(4)]
CORES = [(t, t ^ 1) for t in range(4)]
RETURNS = [(2, 0), (3, 1)]
CROSSED = [(t, t ^ 3) for t in range(4)]
NEVER = -1e30


def ship_kernel(query, key, value, grad, same, other, swap, held, held_swap, sems, out_sems):
    member = lax.axis_index("tm")
    chip, core = member // 2, member % 2
    width = same.shape[-1]
    own_columns = pl.ds(pl.multiple_of(core * width, width), width)
    other_columns = pl.ds(pl.multiple_of((1 - core) * width, width), width)

    def copy_all(first, second, row):
        rows = pl.ds(row, GROUP)
        steps = [
            (ref.at[:, rows, columns], held.at[i, a], out.at[a])
            for i, (columns, out) in enumerate(((other_columns, other), (own_columns, same)))
            for a, ref in enumerate((first, second))
        ]
        steps += [
            (ref.at[:, :, other_columns], held_swap.at[a], swap.at[a])
            for a, ref in enumerate((query, key, value, grad))
        ]
        loads = [
            pltpu.make_async_copy(source, middle, sems.at[i])
            for i, (source, middle, _) in enumerate(steps)
        ]
        stores = [
            pltpu.make_async_copy(middle, target, out_sems.at[i])
            for i, (_, middle, target) in enumerate(steps)
        ]
        for load in loads:
            load.start()
        for load, store in zip(loads, stores):
            load.wait()
            store.start()
        for store in stores:
            store.wait()

    @pl.when(chip == 0)
    def _():
        copy_all(key, value, 0)

    @pl.when(chip == 1)
    def _():
        copy_all(query, grad, GROUP)


def ship_pack(query, key, value, grad):
    frames, positions, width = query.shape
    half = width // 2
    shape = jax.ShapeDtypeStruct((2, frames, GROUP, half), query.dtype)
    swap_shape = jax.ShapeDtypeStruct((4, frames, positions, half), query.dtype)
    return pl.pallas_call(
        ship_kernel,
        in_specs=[pl.BlockSpec(memory_space=pltpu.HBM)] * 4,
        out_specs=[pl.BlockSpec(memory_space=pltpu.HBM)] * 3,
        out_shape=[shape, shape, swap_shape],
        scratch_shapes=[
            pltpu.VMEM((2,) + shape.shape, shape.dtype),
            pltpu.VMEM(swap_shape.shape, shape.dtype),
            pltpu.SemaphoreType.DMA((8,)),
            pltpu.SemaphoreType.DMA((8,)),
        ],
        compiler_params=PARAMS,
        cost_estimate=cost(2),
        name="ship_pack",
    )(query, key, value, grad)


def frame_mask(core, chip_frames, causal):
    rows = chip_frames * GROUP
    half = chip_frames // 2
    key_row = lax.broadcasted_iota(jnp.int32, (rows, rows), 0)
    query_row = lax.broadcasted_iota(jnp.int32, (rows, rows), 1)
    same = key_row % GROUP == query_row % GROUP
    key_frame = (key_row // GROUP + core * half) % chip_frames
    query_frame = (query_row // GROUP + core * half) % chip_frames
    return same & ((key_frame <= query_frame) | jnp.logical_not(causal))


def gather_rows(own, other, row, columns):
    rows = pl.ds(row, GROUP)
    return jnp.concatenate(
        [
            own[:, rows, columns].reshape(-1, HEAD_DIM),
            other[:, rows, columns].reshape(-1, HEAD_DIM),
        ],
        axis=0,
    )


def block_stats(mask, query, key, value, grad):
    scores = dot(key, query, ((1,), (1,))) * (SCALE * LOG2E)
    scores = jnp.where(mask, scores, NEVER)
    peak = jnp.max(scores, axis=0, keepdims=True)
    e = jnp.exp2(scores - peak)
    pgrad = dot(value, grad, ((1,), (1,)))
    return (
        (scores, pgrad),
        (peak, jnp.sum(e, axis=0, keepdims=True), jnp.sum(e * pgrad, axis=0, keepdims=True)),
    )


def block_grads(products, stats, more, query, key, grad):
    scores, pgrad = products
    peak = jnp.maximum(stats[0], more[0])
    own_scale, more_scale = jnp.exp2(stats[0] - peak), jnp.exp2(more[0] - peak)
    inverse = 1.0 / (stats[1] * own_scale + more[1] * more_scale)
    delta = (stats[2] * own_scale + more[2] * more_scale) * inverse
    probs = jnp.exp2(scores - peak) * inverse
    weights = probs.astype(jnp.bfloat16)
    sgrad = (probs * (pgrad - delta)).astype(jnp.bfloat16)
    dquery = dot(sgrad, key, ((0,), (0,))) * SCALE
    dkey = dot(sgrad, query, ((1,), (0,))) * SCALE
    dvalue = dot(weights, grad, ((1,), (0,)))
    return dquery, dkey, dvalue


def stats_kernel(place, query, key, value, grad, swapped, out):
    mask = frame_mask(place[0] % 2, 2 * query.shape[0], True)
    heads = query.shape[-1] // HEAD_DIM
    for h in range(heads):
        columns = pl.ds(h * HEAD_DIM, HEAD_DIM)
        rows = [
            gather_rows(ref, swapped.at[a], 0, columns)
            for a, ref in enumerate((query, key, value, grad))
        ]
        write_stats(out, h, heads, block_stats(mask, *rows)[1])


def write_stats(out, h, heads, stats):
    for i, row in enumerate(stats):
        out[i, pl.ds(pl.program_id(0) * heads + h, 1)] = row


def read_stats(far, h, heads):
    return tuple(far[i, pl.ds(pl.program_id(0) * heads + h, 1)] for i in range(3))


def choose(first, when_first, when_second):
    return tuple(jnp.where(first, a, b) for a, b in zip(when_first, when_second))


def no_stats(rows):
    zero = jnp.zeros((1, rows), jnp.float32)
    return (zero + NEVER, zero, zero)


def place_rows(own, others, a, columns, values):
    values = values.astype(jnp.bfloat16).reshape(2, -1, GROUP, HEAD_DIM)
    own[a, :, :, columns] = values[0]
    others[a, :, :, columns] = values[1]


def early_kernel(
    place, query, key, value, grad, swapped, late_key, late_value, late_swapped, same, other, far,
    early, early_other, near, near_other, back, back_value, stats_out,
):
    core, first = place[0] % 2, place[0] < 2
    frames = query.shape[0]
    causal = frame_mask(core, 2 * frames, True)
    cross = frame_mask(core, 2 * frames, False)
    heads = query.shape[-1] // HEAD_DIM
    for h in range(heads):
        columns = pl.ds(h * HEAD_DIM, HEAD_DIM)
        rows = [
            gather_rows(ref, swapped.at[a], 0, columns)
            for a, ref in enumerate((query, key, value, grad))
        ]
        late = [
            gather_rows(ref, late_swapped.at[a], 0, columns)
            for a, ref in ((1, late_key), (2, late_value))
        ]
        sent = [gather_rows(same.at[a], other.at[a], 0, columns) for a in range(2)]
        crossed = [
            jnp.where(first, sent[0], rows[0]),
            jnp.where(first, late[0], sent[0]),
            jnp.where(first, late[1], sent[1]),
            jnp.where(first, sent[1], rows[3]),
        ]
        received = read_stats(far, h, heads)
        products, stats = block_stats(causal, *rows)
        cross_products, cross_stats = block_stats(cross, *crossed)
        write_stats(stats_out, h, heads, cross_stats)
        none = no_stats(2 * frames * GROUP)
        out = block_grads(
            products, stats, choose(first, none, cross_stats), rows[0], rows[1], rows[3]
        )
        cross_out = block_grads(
            cross_products,
            cross_stats,
            choose(first, received, stats),
            crossed[0],
            crossed[1],
            crossed[3],
        )
        zero = jnp.zeros_like(cross_out[0])
        place_rows(early, early_other, 0, columns, out[0] + jnp.where(first, zero, cross_out[0]))
        place_rows(early, early_other, 1, columns, out[1])
        place_rows(early, early_other, 2, columns, out[2])
        place_rows(near, near_other, 0, columns, cross_out[1])
        place_rows(near, near_other, 1, columns, cross_out[2])
        mixed = jnp.where(first, cross_out[0], cross_out[1])
        place_rows(back.at[0:1], back.at[1:2], 0, columns, mixed)
        place_rows(back_value.at[0:1], back_value.at[1:2], 0, columns, cross_out[2])


def late_kernel(
    place, query, key, value, grad, swapped, far, early, early_other, near, near_other, back,
    back_value, dquery, dkey, dvalue, theirs,
):
    core, first = place[0] % 2, place[0] < 2
    frames = query.shape[0]
    causal = frame_mask(core, 2 * frames, True)
    early_rows, late_rows = pl.ds(0, GROUP), pl.ds(GROUP, GROUP)
    heads = query.shape[-1] // HEAD_DIM
    for h in range(heads):
        columns = pl.ds(h * HEAD_DIM, HEAD_DIM)
        rows = [
            gather_rows(ref, swapped.at[a], 0, columns)
            for a, ref in enumerate((query, key, value, grad))
        ]
        received = read_stats(far, h, heads)
        products, stats = block_stats(causal, *rows)
        none = no_stats(2 * frames * GROUP)
        late = [
            values.reshape(2, frames, GROUP, HEAD_DIM)
            for values in block_grads(
                products, stats, choose(first, none, received), rows[0], rows[1], rows[3]
            )
        ]

        def write(outs, side, near, early):
            zero = jnp.zeros((frames, GROUP, HEAD_DIM), jnp.float32)
            far_rows = [ref[side, :, :, columns].astype(jnp.float32) for ref in (back, back_value)]
            near = [near[a, :, :, columns].astype(jnp.float32) for a in range(2)]
            early = [early[a, :, :, columns].astype(jnp.float32) for a in range(3)]
            early[1] += jnp.where(first, far_rows[0], zero)
            early[2] += jnp.where(first, far_rows[1], zero)
            more = (
                jnp.where(first, zero, far_rows[0]),
                jnp.where(first, near[0], zero),
                jnp.where(first, near[1], zero),
            )
            for a, out in enumerate(outs):
                out[:, early_rows, columns] = early[a].astype(jnp.bfloat16)
                out[:, late_rows, columns] = (late[a][side] + more[a]).astype(jnp.bfloat16)

        write((dquery, dkey, dvalue), 0, near, early)
        write([theirs.at[a] for a in range(3)], 1, near_other, early_other)


def finish_kernel(place, swapped, *refs):
    for a, out in enumerate(refs[3:]):
        out[...] = swapped[a]


STATS_STEPS, EARLY_STEPS, LATE_STEPS, FINISH_STEPS = 2, 4, 4, 4


class Temporal:
    def __init__(self, arrays):
        self.arrays = arrays
        self.frames, self.positions, self.width = arrays[0].shape
        self.half = self.width // 2
        self.heads = self.half // HEAD_DIM
        member = lax.axis_index("tm")
        self.place = member.reshape(1)

    def own(self, steps, row):
        return pl.BlockSpec(
            (self.frames, GROUP, self.half // steps),
            lambda j, p: (0, row, (p[0] % 2) * steps + j),
        )

    def part(self, steps, count, rows, row=0):
        return pl.BlockSpec(
            (count, self.frames, rows, self.half // steps), lambda j, p: (0, 0, row, j)
        )

    def stats(self):
        return pl.BlockSpec(self.stats_shape().shape, lambda j, p: (0, 0, 0))

    def stats_shape(self):
        return jax.ShapeDtypeStruct((3, self.heads, 2 * self.frames * GROUP), jnp.float32)

    def shape(self, count, rows):
        return jax.ShapeDtypeStruct((count, self.frames, rows, self.half), jnp.bfloat16)

    def call(self, steps, kernel, name, micros, in_specs, out_specs, out_shape, operands, params=PARAMS, aliases={}):
        return pl.pallas_call(
            kernel,
            grid_spec=pltpu.PrefetchScalarGridSpec(
                num_scalar_prefetch=1, grid=(steps,), in_specs=in_specs, out_specs=out_specs
            ),
            out_shape=out_shape,
            input_output_aliases=aliases,
            compiler_params=PARAMS,
        cost_estimate=cost(micros),
            name=name,
        )(self.place, *operands)

    def late_stats(self, swapped):
        return self.call(
            STATS_STEPS,
            stats_kernel,
            "temporal_stats",
            5,
            [self.own(STATS_STEPS, 1)] * 4 + [self.part(STATS_STEPS, 4, GROUP, 1)],
            self.stats(),
            self.stats_shape(),
            self.arrays + (swapped,),
        )

    def early_grads(self, swapped, same, other, far):
        return self.call(
            EARLY_STEPS,
            early_kernel,
            "temporal_early",
            EARLY_COST,
            [self.own(EARLY_STEPS, 0)] * 4
            + [self.part(EARLY_STEPS, 4, GROUP)]
            + [self.own(EARLY_STEPS, 1)] * 2
            + [self.part(EARLY_STEPS, 4, GROUP, 1)]
            + [self.part(EARLY_STEPS, 2, GROUP)] * 2
            + [self.stats()],
            [self.part(EARLY_STEPS, 3, GROUP)] * 2 + [self.part(EARLY_STEPS, 2, GROUP)] * 4 + [self.stats()],
            [self.shape(3, GROUP)] * 2 + [self.shape(2, GROUP)] * 4 + [self.stats_shape()],
            self.arrays
            + (swapped, self.arrays[1], self.arrays[2], swapped, same, other, far),
        )

    def late_grads(self, swapped, far, *parts):
        out = pl.BlockSpec(
            (self.frames, self.positions, self.half // LATE_STEPS), lambda j, p: (0, 0, (p[0] % 2) * LATE_STEPS + j)
        )
        out_shape = jax.ShapeDtypeStruct((self.frames, self.positions, self.width), jnp.bfloat16)
        return self.call(
            LATE_STEPS,
            late_kernel,
            "temporal_late",
            LATE_COST,
            [self.own(LATE_STEPS, 1)] * 4
            + [self.part(LATE_STEPS, 4, GROUP, 1), self.stats()]
            + [self.part(LATE_STEPS, 3, GROUP)] * 2
            + [self.part(LATE_STEPS, 2, GROUP)] * 4,
            [out] * 3 + [self.part(LATE_STEPS, 3, self.positions)],
            [out_shape] * 3 + [self.shape(3, self.positions)],
            self.arrays + (swapped, far) + parts,
            LATE_PARAMS,
        )

    def finish(self, outs, swapped):
        out = pl.BlockSpec(
            (self.frames, self.positions, self.half // FINISH_STEPS),
            lambda j, p: (0, 0, (1 - p[0] % 2) * FINISH_STEPS + j),
        )
        return self.call(
            FINISH_STEPS,
            finish_kernel,
            "temporal_finish",
            3,
            [self.part(FINISH_STEPS, 3, self.positions)] + [pl.BlockSpec(memory_space=pl.ANY)] * 3,
            [out] * 3,
            [jax.ShapeDtypeStruct(a.shape, a.dtype) for a in outs],
            (swapped,) + tuple(outs),
            LATE_PARAMS,
            {2: 0, 3: 1, 4: 2},
        )


EARLY_COST = 100
LATE_COST = 100


def local(
    space_query, space_key, space_value, space_grad, time_query, time_key, time_value, time_grad
):
    def flat(array):
        return array.reshape(array.shape[1:])

    def chips(array):
        return lax.ppermute(array, "tm", CHIPS)

    def crossed(array):
        return lax.ppermute(array, "tm", CROSSED)

    def cores(array):
        return lax.ppermute(array, "tm", CORES)

    spatial = tuple(map(flat, (space_query, space_key, space_value, space_grad)))
    arrays = tuple(map(flat, (time_query, time_key, time_value, time_grad)))

    ships, arrays, spatial = lax.optimization_barrier((ship_pack(*arrays), arrays, spatial))
    same, other, swapped = chips(ships[0]), crossed(ships[1]), cores(ships[2])
    work = Temporal(arrays)
    packed, far = lax.optimization_barrier((pack_heads(*spatial), work.late_stats(swapped)))
    far = chips(far)
    packed = lax.all_to_all(packed, "space", 0, 0, tiled=True)
    early, early_other, near, near_other, back, back_value, far = work.early_grads(
        swapped, same, other, far
    )
    far, back, back_value = chips(far), chips(back), lax.ppermute(back_value, "tm", RETURNS)
    packed = lax.all_to_all(spatial_grads(packed), "space", 0, 0, tiled=True)
    *outs, theirs = work.late_grads(
        swapped, far, early, early_other, near, near_other, back, back_value
    )
    outs = work.finish(outs, cores(theirs))
    outs = tuple(unpack_heads(packed)) + tuple(outs)
    return tuple(out.reshape(space_query.shape) for out in outs)


def solution(mesh):
    spec = P(None, "tm", "space", None)
    return jax.shard_map(
        local, mesh=mesh, in_specs=(spec,) * 8, out_specs=(spec,) * 6, check_vma=False
    )
```

```python
import math

import jax
import jax.numpy as jnp
from jax import lax
from jax.experimental import pallas as pl
from jax.experimental.pallas import tpu as pltpu
from jax.sharding import PartitionSpec as P

HEAD_DIM = 128
SCALE = 1.0 / math.sqrt(HEAD_DIM)
LOG2E = 1.0 / math.log(2.0)
MIB = 1024 * 1024
PARAMS = pltpu.CompilerParams(vmem_limit_bytes=60 * MIB)
LATE_PARAMS = pltpu.CompilerParams(vmem_limit_bytes=59 * MIB)
UNPACK_PARAMS = pltpu.CompilerParams(vmem_limit_bytes=16 * MIB)


def cost(micros):
    return pl.CostEstimate(flops=int(micros * 1e9), bytes_accessed=0, transcendentals=0)


def dot(a, b, contract):
    return lax.dot_general(a, b, (contract, ((), ())), preferred_element_type=jnp.float32)


def pack_kernel(*refs):
    *ins, out, rows, heads, row_sems, head_sems = refs
    count, frames = rows.shape[:2]

    def load(f, a):
        return pltpu.make_async_copy(ins[a].at[f], rows.at[a, f], row_sems.at[f, a])

    def store(f):
        return pltpu.make_async_copy(heads.at[:, f], out.at[:, f], head_sems.at[f])

    for f in range(frames):
        for a in range(count):
            load(f, a).start()
    for f in range(frames):
        for a in range(count):
            load(f, a).wait()
            for h in range(heads.shape[0]):
                heads[h, f, a] = rows[a, f, :, h * HEAD_DIM : (h + 1) * HEAD_DIM]
        store(f).start()
    for f in range(frames):
        store(f).wait()


def pack_heads(*arrays):
    frames, positions, width = arrays[0].shape
    count, heads = len(arrays), width // HEAD_DIM
    dtype = arrays[0].dtype
    packed = (heads, frames, count, positions, HEAD_DIM)
    return pl.pallas_call(
        pack_kernel,
        in_specs=[pl.BlockSpec(memory_space=pltpu.HBM)] * count,
        out_specs=pl.BlockSpec(memory_space=pl.ANY),
        out_shape=jax.ShapeDtypeStruct(packed, dtype),
        scratch_shapes=[
            pltpu.VMEM((count, frames, positions, width), dtype),
            pltpu.VMEM(packed, dtype),
            pltpu.SemaphoreType.DMA((frames, count)),
            pltpu.SemaphoreType.DMA((frames,)),
        ],
        compiler_params=PARAMS,
        cost_estimate=cost(5),
        name="pack_heads",
    )(*arrays)


def unpack_kernel(ref, *outs):
    heads = ref.shape[0]
    for a, out in enumerate(outs):
        for h in range(heads):
            out[0, :, h * HEAD_DIM : (h + 1) * HEAD_DIM] = ref[h, 0, a]


def unpack_heads(array):
    heads, frames, count, positions, _ = array.shape
    width = heads * HEAD_DIM
    return pl.pallas_call(
        unpack_kernel,
        grid=(frames,),
        in_specs=[
            pl.BlockSpec((heads, 1, count, positions, HEAD_DIM), lambda f: (0, f, 0, 0, 0))
        ],
        out_specs=[pl.BlockSpec((1, positions, width), lambda f: (f, 0, 0))] * count,
        out_shape=[jax.ShapeDtypeStruct((frames, positions, width), array.dtype)] * count,
        compiler_params=UNPACK_PARAMS,
        cost_estimate=cost(4),
        name="unpack_heads",
    )(array)


def spatial_kernel(ref, out):
    parts, _, _, rows, _ = ref.shape
    query, key, value, grad = (ref[:, 0, a].reshape(parts * rows, HEAD_DIM) for a in range(4))
    scores = dot(query, key, ((1,), (1,)))
    peak = jnp.max(scores, axis=1, keepdims=True)
    e = jnp.exp2((scores - peak) * (SCALE * LOG2E))
    pgrad = dot(grad, value, ((1,), (1,)))
    probs = e * (1.0 / jnp.sum(e, axis=1, keepdims=True))
    term = probs * pgrad
    delta = jnp.sum(term, axis=1, keepdims=True)
    sgrad = (term - probs * delta).astype(jnp.bfloat16)
    results = (
        dot(sgrad, key, ((1,), (0,))) * SCALE,
        dot(query.T, sgrad, ((1,), (0,))).T * SCALE,
        dot(grad.T, probs.astype(jnp.bfloat16), ((1,), (0,))).T,
    )
    for a, result in enumerate(results):
        out[:, 0, a] = result.astype(out.dtype).reshape(parts, rows, HEAD_DIM)


def spatial_grads(array):
    parts, frames, _, rows, _ = array.shape
    return pl.pallas_call(
        spatial_kernel,
        grid=(frames,),
        in_specs=[pl.BlockSpec((parts, 1, 4, rows, HEAD_DIM), lambda f: (0, f, 0, 0, 0))],
        out_specs=pl.BlockSpec((parts, 1, 3, rows, HEAD_DIM), lambda f: (0, f, 0, 0, 0)),
        out_shape=jax.ShapeDtypeStruct((parts, frames, 3, rows, HEAD_DIM), array.dtype),
        compiler_params=PARAMS,
        cost_estimate=cost(20),
        name="spatial_grads",
    )(array)


GROUP = 16
CHIPS = [(t, t ^ 2) for t in range(4)]
CORES = [(t, t ^ 1) for t in range(4)]
CROSSED = [(t, t ^ 3) for t in range(4)]
NEVER = -1e30


def copy_through(steps, sems, out_sems):
    loads = [
        pltpu.make_async_copy(source, middle, sems.at[i])
        for i, (source, middle, _) in enumerate(steps)
    ]
    stores = [
        pltpu.make_async_copy(middle, target, out_sems.at[i])
        for i, (_, middle, target) in enumerate(steps)
    ]
    for load in loads:
        load.start()
    for load, store in zip(loads, stores):
        load.wait()
        store.start()
    for store in stores:
        store.wait()


def half_columns(core, width):
    return pl.ds(pl.multiple_of(core * width, width), width)


def ship_kernel(query, key, value, grad, same, other, swap, held, held_swap, sems, out_sems):
    member = lax.axis_index("tm")
    chip, core = member // 2, member % 2
    width = same.shape[-1]
    own, others = half_columns(core, width), half_columns(1 - core, width)

    def copy_all(first, second, row):
        rows = pl.ds(row, GROUP)
        steps = [
            (ref.at[:, rows, columns], held.at[i, a], out.at[a])
            for i, (columns, out) in enumerate(((others, other), (own, same)))
            for a, ref in enumerate((first, second))
        ]
        steps += [
            (ref.at[:, :, others], held_swap.at[a], swap.at[a])
            for a, ref in enumerate((query, key, value, grad))
        ]
        copy_through(steps, sems, out_sems)

    @pl.when(chip == 0)
    def _():
        copy_all(key, value, 0)

    @pl.when(chip == 1)
    def _():
        copy_all(query, grad, GROUP)


def ship_pack(*arrays):
    frames, positions, width = arrays[0].shape
    dtype = arrays[0].dtype
    shape = jax.ShapeDtypeStruct((2, frames, GROUP, width // 2), dtype)
    swap_shape = jax.ShapeDtypeStruct((4, frames, positions, width // 2), dtype)
    hbm = pl.BlockSpec(memory_space=pltpu.HBM)
    return pl.pallas_call(
        ship_kernel,
        in_specs=[hbm] * 4,
        out_specs=[hbm] * 3,
        out_shape=[shape, shape, swap_shape],
        scratch_shapes=[
            pltpu.VMEM((2,) + shape.shape, dtype),
            pltpu.VMEM(swap_shape.shape, dtype),
            pltpu.SemaphoreType.DMA((8,)),
            pltpu.SemaphoreType.DMA((8,)),
        ],
        compiler_params=PARAMS,
        cost_estimate=cost(2),
        name="ship_pack",
    )(*arrays)


def frame_mask(core, chip_frames, causal):
    rows = chip_frames * GROUP
    half = chip_frames // 2
    key_row = lax.broadcasted_iota(jnp.int32, (rows, rows), 0)
    query_row = lax.broadcasted_iota(jnp.int32, (rows, rows), 1)
    same = key_row % GROUP == query_row % GROUP
    key_frame = (key_row // GROUP + core * half) % chip_frames
    query_frame = (query_row // GROUP + core * half) % chip_frames
    return same & ((key_frame <= query_frame) | jnp.logical_not(causal))


def gather_rows(own, other, row, columns):
    rows = pl.ds(row, GROUP)
    return jnp.concatenate(
        [
            own[:, rows, columns].reshape(-1, HEAD_DIM),
            other[:, rows, columns].reshape(-1, HEAD_DIM),
        ],
        axis=0,
    )


def block_stats(mask, query, key, value, grad):
    scores = dot(key, query, ((1,), (1,))) * (SCALE * LOG2E)
    scores = jnp.where(mask, scores, NEVER)
    peak = jnp.max(scores, axis=0, keepdims=True)
    e = jnp.exp2(scores - peak)
    pgrad = dot(value, grad, ((1,), (1,)))
    return (
        (scores, pgrad),
        (peak, jnp.sum(e, axis=0, keepdims=True), jnp.sum(e * pgrad, axis=0, keepdims=True)),
    )


def merged(stats, more):
    peak = jnp.maximum(stats[0], more[0])
    own_scale, more_scale = jnp.exp2(stats[0] - peak), jnp.exp2(more[0] - peak)
    inverse = 1.0 / (stats[1] * own_scale + more[1] * more_scale)
    return peak, inverse, (stats[2] * own_scale + more[2] * more_scale) * inverse


def block_weights(products, stats, more):
    scores, pgrad = products
    peak, inverse, delta = merged(stats, more)
    probs = jnp.exp2(scores - peak) * inverse
    return probs.astype(jnp.bfloat16), (probs * (pgrad - delta)).astype(jnp.bfloat16)


def block_grads(weights, sgrad, query, key, grad):
    dquery = dot(sgrad, key, ((0,), (0,))) * SCALE
    dkey = dot(sgrad, query, ((1,), (0,))) * SCALE
    dvalue = dot(weights, grad, ((1,), (0,)))
    return dquery, dkey, dvalue


def write_stats(out, h, heads, stats):
    for i, row in enumerate(stats):
        out[i, pl.ds(pl.program_id(0) * heads + h, 1)] = row


def read_stats(far, h, heads):
    return tuple(far[i, pl.ds(pl.program_id(0) * heads + h, 1)] for i in range(3))


def choose(first, when_first, when_second):
    return tuple(jnp.where(first, a, b) for a, b in zip(when_first, when_second))


def no_stats(rows):
    zero = jnp.zeros((1, rows), jnp.float32)
    return (zero + NEVER, zero, zero)


def place_rows(own, others, a, columns, values):
    values = values.astype(jnp.bfloat16).reshape(2, -1, GROUP, HEAD_DIM)
    own[a, :, :, columns] = values[0]
    others[a, :, :, columns] = values[1]


def load_rows(refs, swapped, columns):
    return [gather_rows(ref, swapped.at[a], 0, columns) for a, ref in enumerate(refs)]


def early_kernel(
    place, query, key, value, grad, swapped, late_query, late_key, late_value, late_grad,
    late_swapped, same, other, early, early_other, back, stats_out,
):
    core, first = place[0] % 2, place[0] < 2
    frames = query.shape[0]
    causal = frame_mask(core, 2 * frames, True)
    cross = frame_mask(core, 2 * frames, False)
    none = no_stats(2 * frames * GROUP)
    heads = query.shape[-1] // HEAD_DIM
    for h in range(heads):
        columns = pl.ds(h * HEAD_DIM, HEAD_DIM)
        rows = load_rows((query, key, value, grad), swapped, columns)
        late = load_rows((late_query, late_key, late_value, late_grad), late_swapped, columns)
        sent = [gather_rows(same.at[a], other.at[a], 0, columns) for a in range(2)]
        crossed = [
            jnp.where(first, sent[0], rows[0]),
            jnp.where(first, late[1], sent[0]),
            jnp.where(first, late[2], sent[1]),
            jnp.where(first, sent[1], rows[3]),
        ]
        products, stats = block_stats(causal, *rows)
        cross_products, cross_stats = block_stats(cross, *crossed)
        late_stats = block_stats(causal, *late)[1]
        write_stats(stats_out, h, heads, choose(first, cross_stats, late_stats))
        out = block_grads(
            *block_weights(products, stats, choose(first, none, cross_stats)),
            rows[0],
            rows[1],
            rows[3],
        )
        cross_weights, cross_sgrad = block_weights(
            cross_products, cross_stats, choose(first, none, stats)
        )
        cross_out = block_grads(cross_weights, cross_sgrad, crossed[0], crossed[1], crossed[3])
        mean_key = dot(cross_weights, crossed[1], ((0,), (0,))) * SCALE
        zero = jnp.zeros_like(mean_key)
        place_rows(early, early_other, 0, columns, out[0] + jnp.where(first, zero, cross_out[0]))
        place_rows(early, early_other, 1, columns, out[1])
        place_rows(early, early_other, 2, columns, out[2])
        returns = (
            jnp.where(first, cross_out[0], cross_out[1]),
            jnp.where(first, mean_key, cross_out[2]),
        )
        for a, values in enumerate(returns):
            place_rows(back.at[0:2], back.at[2:4], a, columns, values)


def late_kernel(
    place, query, key, value, grad, swapped, same, other, far, early, early_other, back,
    dquery, dkey, dvalue, theirs,
):
    core, first = place[0] % 2, place[0] < 2
    frames = query.shape[0]
    causal = frame_mask(core, 2 * frames, True)
    cross = frame_mask(core, 2 * frames, False)
    early_rows, late_rows = pl.ds(0, GROUP), pl.ds(GROUP, GROUP)
    none = no_stats(2 * frames * GROUP)
    heads = query.shape[-1] // HEAD_DIM
    for h in range(heads):
        columns = pl.ds(h * HEAD_DIM, HEAD_DIM)
        rows = load_rows((query, key, value, grad), swapped, columns)
        sent = [gather_rows(same.at[a], other.at[a], 0, columns) for a in range(2)]
        received = read_stats(far, h, heads)
        products, stats = block_stats(causal, *rows)
        more = choose(first, none, received)
        late = block_grads(*block_weights(products, stats, more), rows[0], rows[1], rows[3])

        cross_products, cross_stats = block_stats(cross, sent[0], rows[1], rows[2], sent[1])
        weights, sgrad = block_weights(cross_products, cross_stats, received)
        near_key = dot(sgrad, sent[0], ((1,), (0,))) * SCALE
        near_value = dot(weights, sent[1], ((1,), (0,)))

        peak, inverse, delta = merged(stats, received)
        share = received[1] * jnp.exp2(received[0] - peak) * inverse
        shift = share * (delta - received[2] / received[1])
        factors = jnp.concatenate(
            [share, shift, jnp.zeros((6, share.shape[1]), jnp.float32)], axis=0
        ).T
        far_rows = [
            jnp.concatenate(
                [back[side * 2 + a, :, :, columns].reshape(-1, HEAD_DIM) for side in range(2)],
                axis=0,
            ).astype(jnp.float32)
            for a in range(2)
        ]
        far_query = far_rows[0] * factors[:, 0:1] - far_rows[1] * factors[:, 1:2]
        zero = jnp.zeros_like(far_query)
        late = [
            late[0] + jnp.where(first, zero, far_query),
            late[1] + jnp.where(first, near_key, zero),
            late[2] + jnp.where(first, near_value, zero),
        ]
        late = [values.reshape(2, frames, GROUP, HEAD_DIM) for values in late]
        far_rows = [
            jnp.where(first, values, zero).reshape(2, frames, GROUP, HEAD_DIM)
            for values in far_rows
        ]

        def write(outs, side, early):
            for a, out in enumerate(outs):
                sums = early[a, :, :, columns].astype(jnp.float32)
                if a > 0:
                    sums += far_rows[a - 1][side]
                out[:, early_rows, columns] = sums.astype(jnp.bfloat16)
                out[:, late_rows, columns] = late[a][side].astype(jnp.bfloat16)

        write((dquery, dkey, dvalue), 0, early)
        write([theirs.at[a] for a in range(3)], 1, early_other)


def finish_kernel(place, swapped, *refs):
    for a, out in enumerate(refs[3:]):
        out[...] = swapped[a]


EARLY_STEPS, LATE_STEPS, FINISH_STEPS = 4, 4, 4


class Temporal:
    def __init__(self, arrays):
        self.arrays = arrays
        self.frames, self.positions, self.width = arrays[0].shape
        self.half = self.width // 2
        self.heads = self.half // HEAD_DIM
        member = lax.axis_index("tm")
        self.place = member.reshape(1)

    def own(self, steps, row):
        return pl.BlockSpec(
            (self.frames, GROUP, self.half // steps),
            lambda j, p: (0, row, (p[0] % 2) * steps + j),
        )

    def part(self, steps, count, rows, row=0):
        return pl.BlockSpec(
            (count, self.frames, rows, self.half // steps), lambda j, p: (0, 0, row, j)
        )

    def stats(self):
        return pl.BlockSpec(self.stats_shape().shape, lambda j, p: (0, 0, 0))

    def stats_shape(self):
        return jax.ShapeDtypeStruct((3, self.heads, 2 * self.frames * GROUP), jnp.float32)

    def shape(self, count, rows):
        return jax.ShapeDtypeStruct((count, self.frames, rows, self.half), jnp.bfloat16)

    def call(self, steps, kernel, name, micros, in_specs, out_specs, out_shape, operands, params=PARAMS, aliases={}):
        return pl.pallas_call(
            kernel,
            grid_spec=pltpu.PrefetchScalarGridSpec(
                num_scalar_prefetch=1, grid=(steps,), in_specs=in_specs, out_specs=out_specs
            ),
            out_shape=out_shape,
            input_output_aliases=aliases,
            compiler_params=PARAMS,
        cost_estimate=cost(micros),
            name=name,
        )(self.place, *operands)

    def early_grads(self, swapped, same, other):
        return self.call(
            EARLY_STEPS,
            early_kernel,
            "temporal_early",
            EARLY_COST,
            [self.own(EARLY_STEPS, 0)] * 4
            + [self.part(EARLY_STEPS, 4, GROUP)]
            + [self.own(EARLY_STEPS, 1)] * 4
            + [self.part(EARLY_STEPS, 4, GROUP, 1)]
            + [self.part(EARLY_STEPS, 2, GROUP)] * 2,
            [self.part(EARLY_STEPS, 3, GROUP)] * 2
            + [self.part(EARLY_STEPS, 4, GROUP), self.stats()],
            [self.shape(3, GROUP)] * 2 + [self.shape(4, GROUP), self.stats_shape()],
            self.arrays + (swapped,) + self.arrays + (swapped, same, other),
        )

    def late_grads(self, swapped, same, other, far, *parts):
        out = pl.BlockSpec(
            (self.frames, self.positions, self.half // LATE_STEPS),
            lambda j, p: (0, 0, (p[0] % 2) * LATE_STEPS + j),
        )
        out_shape = jax.ShapeDtypeStruct((self.frames, self.positions, self.width), jnp.bfloat16)
        return self.call(
            LATE_STEPS,
            late_kernel,
            "temporal_late",
            LATE_COST,
            [self.own(LATE_STEPS, 1)] * 4
            + [self.part(LATE_STEPS, 4, GROUP, 1)]
            + [self.part(LATE_STEPS, 2, GROUP)] * 2
            + [self.stats()]
            + [self.part(LATE_STEPS, 3, GROUP)] * 2
            + [self.part(LATE_STEPS, 4, GROUP)],
            [out] * 3 + [self.part(LATE_STEPS, 3, self.positions)],
            [out_shape] * 3 + [self.shape(3, self.positions)],
            self.arrays + (swapped, same, other, far) + parts,
            LATE_PARAMS,
        )

    def finish(self, outs, swapped):
        out = pl.BlockSpec(
            (self.frames, self.positions, self.half // FINISH_STEPS),
            lambda j, p: (0, 0, (1 - p[0] % 2) * FINISH_STEPS + j),
        )
        return self.call(
            FINISH_STEPS,
            finish_kernel,
            "temporal_finish",
            3,
            [self.part(FINISH_STEPS, 3, self.positions)] + [pl.BlockSpec(memory_space=pl.ANY)] * 3,
            [out] * 3,
            [jax.ShapeDtypeStruct(a.shape, a.dtype) for a in outs],
            (swapped,) + tuple(outs),
            LATE_PARAMS,
            {2: 0, 3: 1, 4: 2},
        )


EARLY_COST = 100
LATE_COST = 100


def local(
    space_query, space_key, space_value, space_grad, time_query, time_key, time_value, time_grad
):
    def flat(array):
        return array.reshape(array.shape[1:])

    def chips(array):
        return lax.ppermute(array, "tm", CHIPS)

    def crossed(array):
        return lax.ppermute(array, "tm", CROSSED)

    def cores(array):
        return lax.ppermute(array, "tm", CORES)

    spatial = tuple(map(flat, (space_query, space_key, space_value, space_grad)))
    arrays = tuple(map(flat, (time_query, time_key, time_value, time_grad)))

    ships, arrays, spatial = lax.optimization_barrier((ship_pack(*arrays), arrays, spatial))
    same, other, swapped = chips(ships[0]), crossed(ships[1]), cores(ships[2])
    packed, swapped = lax.optimization_barrier((pack_heads(*spatial), swapped))
    packed = lax.all_to_all(packed, "space", 0, 0, tiled=True)
    work = Temporal(arrays)
    early, early_other, back, far = work.early_grads(swapped, same, other)
    far, back = chips(far), chips(back)
    packed = lax.all_to_all(spatial_grads(packed), "space", 0, 0, tiled=True)
    *outs, theirs = work.late_grads(swapped, same, other, far, early, early_other, back)
    outs = work.finish(outs, cores(theirs))
    outs = tuple(unpack_heads(packed)) + tuple(outs)
    return tuple(out.reshape(space_query.shape) for out in outs)


def solution(mesh):
    spec = P(None, "tm", "space", None)
    return jax.shard_map(
        local, mesh=mesh, in_specs=(spec,) * 8, out_specs=(spec,) * 6, check_vma=False
    )
```

```python
import math

import jax
import jax.numpy as jnp
from jax import lax
from jax.experimental import pallas as pl
from jax.experimental.pallas import tpu as pltpu
from jax.sharding import PartitionSpec as P

HEAD_DIM = 128
SCALE = 1.0 / math.sqrt(HEAD_DIM)
LOG2E = 1.0 / math.log(2.0)
MIB = 1024 * 1024
PARAMS = pltpu.CompilerParams(vmem_limit_bytes=60 * MIB)
LATE_PARAMS = pltpu.CompilerParams(vmem_limit_bytes=59 * MIB)
UNPACK_PARAMS = pltpu.CompilerParams(vmem_limit_bytes=16 * MIB)


def cost(micros):
    return pl.CostEstimate(flops=int(micros * 1e9), bytes_accessed=0, transcendentals=0)


def dot(a, b, contract):
    return lax.dot_general(a, b, (contract, ((), ())), preferred_element_type=jnp.float32)


def pack_kernel(*refs):
    *ins, out, rows, heads, row_sems, head_sems = refs
    count, frames = rows.shape[:2]

    def load(f, a):
        return pltpu.make_async_copy(ins[a].at[f], rows.at[a, f], row_sems.at[f, a])

    def store(f):
        return pltpu.make_async_copy(heads.at[:, f], out.at[:, f], head_sems.at[f])

    for f in range(frames):
        for a in range(count):
            load(f, a).start()
    for f in range(frames):
        for a in range(count):
            load(f, a).wait()
            for h in range(heads.shape[0]):
                heads[h, f, a] = rows[a, f, :, h * HEAD_DIM : (h + 1) * HEAD_DIM]
        store(f).start()
    for f in range(frames):
        store(f).wait()


def pack_heads(*arrays):
    frames, positions, width = arrays[0].shape
    count, heads = len(arrays), width // HEAD_DIM
    dtype = arrays[0].dtype
    packed = (heads, frames, count, positions, HEAD_DIM)
    return pl.pallas_call(
        pack_kernel,
        in_specs=[pl.BlockSpec(memory_space=pltpu.HBM)] * count,
        out_specs=pl.BlockSpec(memory_space=pl.ANY),
        out_shape=jax.ShapeDtypeStruct(packed, dtype),
        scratch_shapes=[
            pltpu.VMEM((count, frames, positions, width), dtype),
            pltpu.VMEM(packed, dtype),
            pltpu.SemaphoreType.DMA((frames, count)),
            pltpu.SemaphoreType.DMA((frames,)),
        ],
        compiler_params=PARAMS,
        cost_estimate=cost(5),
        name="pack_heads",
    )(*arrays)


def unpack_kernel(ref, *refs):
    *outs, rows, sems = refs
    count, frames = rows.shape[:2]
    copies = []
    for f in range(frames):
        for a in range(count):
            for h in range(ref.shape[0]):
                rows[a, f, :, h * HEAD_DIM : (h + 1) * HEAD_DIM] = ref[h, f, a]
            copies.append(pltpu.make_async_copy(rows.at[a, f], outs[a].at[f], sems.at[f, a]))
            copies[-1].start()
    for copy in copies:
        copy.wait()


def unpack_heads(array):
    heads, frames, count, positions, _ = array.shape
    shape = (frames, positions, heads * HEAD_DIM)
    return pl.pallas_call(
        unpack_kernel,
        in_specs=[pl.BlockSpec(memory_space=pltpu.VMEM)],
        out_specs=[pl.BlockSpec(memory_space=pltpu.HBM)] * count,
        out_shape=[jax.ShapeDtypeStruct(shape, array.dtype)] * count,
        scratch_shapes=[
            pltpu.VMEM((count,) + shape, array.dtype),
            pltpu.SemaphoreType.DMA((frames, count)),
        ],
        compiler_params=UNPACK_PARAMS,
        cost_estimate=cost(4),
        name="unpack_heads",
    )(array)


def spatial_kernel(ref, out):
    parts, _, _, rows, _ = ref.shape
    query, key, value, grad = (ref[:, 0, a].reshape(parts * rows, HEAD_DIM) for a in range(4))
    scores = dot(query, key, ((1,), (1,)))
    peak = jnp.max(scores, axis=1, keepdims=True)
    e = jnp.exp2((scores - peak) * (SCALE * LOG2E))
    pgrad = dot(grad, value, ((1,), (1,)))
    probs = e * (1.0 / jnp.sum(e, axis=1, keepdims=True))
    term = probs * pgrad
    delta = jnp.sum(term, axis=1, keepdims=True)
    sgrad = (term - probs * delta).astype(jnp.bfloat16)
    results = (
        dot(sgrad, key, ((1,), (0,))) * SCALE,
        dot(query.T, sgrad, ((1,), (0,))).T * SCALE,
        dot(grad.T, probs.astype(jnp.bfloat16), ((1,), (0,))).T,
    )
    for a, result in enumerate(results):
        out[:, 0, a] = result.astype(out.dtype).reshape(parts, rows, HEAD_DIM)


def spatial_grads(array):
    parts, frames, _, rows, _ = array.shape
    return pl.pallas_call(
        spatial_kernel,
        grid=(frames,),
        in_specs=[pl.BlockSpec((parts, 1, 4, rows, HEAD_DIM), lambda f: (0, f, 0, 0, 0))],
        out_specs=pl.BlockSpec((parts, 1, 3, rows, HEAD_DIM), lambda f: (0, f, 0, 0, 0)),
        out_shape=jax.ShapeDtypeStruct((parts, frames, 3, rows, HEAD_DIM), array.dtype),
        compiler_params=PARAMS,
        cost_estimate=cost(20),
        name="spatial_grads",
    )(array)


GROUP = 16
CHIPS = [(t, t ^ 2) for t in range(4)]
CORES = [(t, t ^ 1) for t in range(4)]
CROSSED = [(t, t ^ 3) for t in range(4)]
NEVER = -1e30


def copy_through(steps, sems, out_sems):
    loads = [
        pltpu.make_async_copy(source, middle, sems.at[i])
        for i, (source, middle, _) in enumerate(steps)
    ]
    stores = [
        pltpu.make_async_copy(middle, target, out_sems.at[i])
        for i, (_, middle, target) in enumerate(steps)
    ]
    for load in loads:
        load.start()
    for load, store in zip(loads, stores):
        load.wait()
        store.start()
    for store in stores:
        store.wait()


def half_columns(core, width):
    return pl.ds(pl.multiple_of(core * width, width), width)


def ship_kernel(query, key, value, grad, same, other, swap, held, held_swap, sems, out_sems):
    member = lax.axis_index("tm")
    chip, core = member // 2, member % 2
    width = same.shape[-1]
    own, others = half_columns(core, width), half_columns(1 - core, width)

    def copy_all(first, second, row):
        rows = pl.ds(row, GROUP)
        steps = [
            (ref.at[:, rows, columns], held.at[i, a], out.at[a])
            for i, (columns, out) in enumerate(((others, other), (own, same)))
            for a, ref in enumerate((first, second))
        ]
        steps += [
            (ref.at[:, :, others], held_swap.at[a], swap.at[a])
            for a, ref in enumerate((query, key, value, grad))
        ]
        copy_through(steps, sems, out_sems)

    @pl.when(chip == 0)
    def _():
        copy_all(key, value, 0)

    @pl.when(chip == 1)
    def _():
        copy_all(query, grad, GROUP)


def ship_pack(*arrays):
    frames, positions, width = arrays[0].shape
    dtype = arrays[0].dtype
    shape = jax.ShapeDtypeStruct((2, frames, GROUP, width // 2), dtype)
    swap_shape = jax.ShapeDtypeStruct((4, frames, positions, width // 2), dtype)
    hbm = pl.BlockSpec(memory_space=pltpu.HBM)
    return pl.pallas_call(
        ship_kernel,
        in_specs=[hbm] * 4,
        out_specs=[hbm] * 3,
        out_shape=[shape, shape, swap_shape],
        scratch_shapes=[
            pltpu.VMEM((2,) + shape.shape, dtype),
            pltpu.VMEM(swap_shape.shape, dtype),
            pltpu.SemaphoreType.DMA((8,)),
            pltpu.SemaphoreType.DMA((8,)),
        ],
        compiler_params=PARAMS,
        cost_estimate=cost(2),
        name="ship_pack",
    )(*arrays)


def frame_mask(core, chip_frames, causal):
    rows = chip_frames * GROUP
    half = chip_frames // 2
    key_row = lax.broadcasted_iota(jnp.int32, (rows, rows), 0)
    query_row = lax.broadcasted_iota(jnp.int32, (rows, rows), 1)
    same = key_row % GROUP == query_row % GROUP
    key_frame = (key_row // GROUP + core * half) % chip_frames
    query_frame = (query_row // GROUP + core * half) % chip_frames
    return same & ((key_frame <= query_frame) | jnp.logical_not(causal))


def gather_rows(own, other, row, columns):
    rows = pl.ds(row, GROUP)
    return jnp.concatenate(
        [
            own[:, rows, columns].reshape(-1, HEAD_DIM),
            other[:, rows, columns].reshape(-1, HEAD_DIM),
        ],
        axis=0,
    )


def block_stats(mask, query, key, value, grad):
    scores = dot(key, query, ((1,), (1,))) * (SCALE * LOG2E)
    scores = jnp.where(mask, scores, NEVER)
    peak = jnp.max(scores, axis=0, keepdims=True)
    e = jnp.exp2(scores - peak)
    pgrad = dot(value, grad, ((1,), (1,)))
    return (
        (scores, pgrad),
        (peak, jnp.sum(e, axis=0, keepdims=True), jnp.sum(e * pgrad, axis=0, keepdims=True)),
    )


def merged(stats, more):
    peak = jnp.maximum(stats[0], more[0])
    own_scale, more_scale = jnp.exp2(stats[0] - peak), jnp.exp2(more[0] - peak)
    inverse = 1.0 / (stats[1] * own_scale + more[1] * more_scale)
    return peak, inverse, (stats[2] * own_scale + more[2] * more_scale) * inverse


def block_weights(products, stats, more):
    scores, pgrad = products
    peak, inverse, delta = merged(stats, more)
    probs = jnp.exp2(scores - peak) * inverse
    return probs.astype(jnp.bfloat16), (probs * (pgrad - delta)).astype(jnp.bfloat16)


def block_grads(weights, sgrad, query, key, grad):
    dquery = dot(sgrad, key, ((0,), (0,))) * SCALE
    dkey = dot(sgrad, query, ((1,), (0,))) * SCALE
    dvalue = dot(weights, grad, ((1,), (0,)))
    return dquery, dkey, dvalue


def write_stats(out, h, heads, stats):
    for i, row in enumerate(stats):
        out[i, pl.ds(pl.program_id(0) * heads + h, 1)] = row


def read_stats(far, h, heads):
    return tuple(far[i, pl.ds(pl.program_id(0) * heads + h, 1)] for i in range(3))


def choose(first, when_first, when_second):
    return tuple(jnp.where(first, a, b) for a, b in zip(when_first, when_second))


def no_stats(rows):
    zero = jnp.zeros((1, rows), jnp.float32)
    return (zero + NEVER, zero, zero)


def place_rows(own, others, a, columns, values):
    values = values.astype(jnp.bfloat16).reshape(2, -1, GROUP, HEAD_DIM)
    own[a, :, :, columns] = values[0]
    others[a, :, :, columns] = values[1]


def load_rows(refs, swapped, columns):
    return [gather_rows(ref, swapped.at[a], 0, columns) for a, ref in enumerate(refs)]


def early_kernel(
    place, query, key, value, grad, swapped, late_query, late_key, late_value, late_grad,
    late_swapped, same, other, early, early_other, back, stats_out,
):
    core, first = place[0] % 2, place[0] < 2
    frames = query.shape[0]
    causal = frame_mask(core, 2 * frames, True)
    cross = frame_mask(core, 2 * frames, False)
    none = no_stats(2 * frames * GROUP)
    heads = query.shape[-1] // HEAD_DIM
    for h in range(heads):
        columns = pl.ds(h * HEAD_DIM, HEAD_DIM)
        rows = load_rows((query, key, value, grad), swapped, columns)
        late = load_rows((late_query, late_key, late_value, late_grad), late_swapped, columns)
        sent = [gather_rows(same.at[a], other.at[a], 0, columns) for a in range(2)]
        crossed = [
            jnp.where(first, sent[0], rows[0]),
            jnp.where(first, late[1], sent[0]),
            jnp.where(first, late[2], sent[1]),
            jnp.where(first, sent[1], rows[3]),
        ]
        products, stats = block_stats(causal, *rows)
        cross_products, cross_stats = block_stats(cross, *crossed)
        late_stats = block_stats(causal, *late)[1]
        write_stats(stats_out, h, heads, choose(first, cross_stats, late_stats))
        out = block_grads(
            *block_weights(products, stats, choose(first, none, cross_stats)),
            rows[0],
            rows[1],
            rows[3],
        )
        cross_weights, cross_sgrad = block_weights(
            cross_products, cross_stats, choose(first, none, stats)
        )
        cross_out = block_grads(cross_weights, cross_sgrad, crossed[0], crossed[1], crossed[3])
        mean_key = dot(cross_weights, crossed[1], ((0,), (0,))) * SCALE
        zero = jnp.zeros_like(mean_key)
        place_rows(early, early_other, 0, columns, out[0] + jnp.where(first, zero, cross_out[0]))
        place_rows(early, early_other, 1, columns, out[1])
        place_rows(early, early_other, 2, columns, out[2])
        returns = (
            jnp.where(first, cross_out[0], cross_out[1]),
            jnp.where(first, mean_key, cross_out[2]),
        )
        for a, values in enumerate(returns):
            place_rows(back.at[0:2], back.at[2:4], a, columns, values)


def late_kernel(
    place, query, key, value, grad, swapped, same, other, far, early, early_other, back,
    dquery, dkey, dvalue, theirs,
):
    core, first = place[0] % 2, place[0] < 2
    frames = query.shape[0]
    causal = frame_mask(core, 2 * frames, True)
    cross = frame_mask(core, 2 * frames, False)
    early_rows, late_rows = pl.ds(0, GROUP), pl.ds(GROUP, GROUP)
    none = no_stats(2 * frames * GROUP)
    heads = query.shape[-1] // HEAD_DIM
    for h in range(heads):
        columns = pl.ds(h * HEAD_DIM, HEAD_DIM)
        rows = load_rows((query, key, value, grad), swapped, columns)
        sent = [gather_rows(same.at[a], other.at[a], 0, columns) for a in range(2)]
        received = read_stats(far, h, heads)
        products, stats = block_stats(causal, *rows)
        more = choose(first, none, received)
        late = block_grads(*block_weights(products, stats, more), rows[0], rows[1], rows[3])

        cross_products, cross_stats = block_stats(cross, sent[0], rows[1], rows[2], sent[1])
        weights, sgrad = block_weights(cross_products, cross_stats, received)
        near_key = dot(sgrad, sent[0], ((1,), (0,))) * SCALE
        near_value = dot(weights, sent[1], ((1,), (0,)))

        peak, inverse, delta = merged(stats, received)
        share = received[1] * jnp.exp2(received[0] - peak) * inverse
        shift = share * (delta - received[2] / received[1])
        factors = jnp.concatenate(
            [share, shift, jnp.zeros((6, share.shape[1]), jnp.float32)], axis=0
        ).T
        far_rows = [
            jnp.concatenate(
                [back[side * 2 + a, :, :, columns].reshape(-1, HEAD_DIM) for side in range(2)],
                axis=0,
            ).astype(jnp.float32)
            for a in range(2)
        ]
        far_query = far_rows[0] * factors[:, 0:1] - far_rows[1] * factors[:, 1:2]
        zero = jnp.zeros_like(far_query)
        late = [
            late[0] + jnp.where(first, zero, far_query),
            late[1] + jnp.where(first, near_key, zero),
            late[2] + jnp.where(first, near_value, zero),
        ]
        late = [values.reshape(2, frames, GROUP, HEAD_DIM) for values in late]
        far_rows = [
            jnp.where(first, values, zero).reshape(2, frames, GROUP, HEAD_DIM)
            for values in far_rows
        ]

        def write(outs, side, early):
            for a, out in enumerate(outs):
                sums = early[a, :, :, columns].astype(jnp.float32)
                if a > 0:
                    sums += far_rows[a - 1][side]
                out[:, early_rows, columns] = sums.astype(jnp.bfloat16)
                out[:, late_rows, columns] = late[a][side].astype(jnp.bfloat16)

        write((dquery, dkey, dvalue), 0, early)
        write([theirs.at[a] for a in range(3)], 1, early_other)


def finish_kernel(place, swapped, *refs):
    for a, out in enumerate(refs[3:]):
        out[...] = swapped[a]


EARLY_STEPS, LATE_STEPS, FINISH_STEPS = 4, 4, 4


class Temporal:
    def __init__(self, arrays):
        self.arrays = arrays
        self.frames, self.positions, self.width = arrays[0].shape
        self.half = self.width // 2
        self.heads = self.half // HEAD_DIM
        member = lax.axis_index("tm")
        self.place = member.reshape(1)

    def own(self, steps, row):
        return pl.BlockSpec(
            (self.frames, GROUP, self.half // steps),
            lambda j, p: (0, row, (p[0] % 2) * steps + j),
        )

    def part(self, steps, count, rows, row=0):
        return pl.BlockSpec(
            (count, self.frames, rows, self.half // steps), lambda j, p: (0, 0, row, j)
        )

    def stats(self):
        return pl.BlockSpec(self.stats_shape().shape, lambda j, p: (0, 0, 0))

    def stats_shape(self):
        return jax.ShapeDtypeStruct((3, self.heads, 2 * self.frames * GROUP), jnp.float32)

    def shape(self, count, rows):
        return jax.ShapeDtypeStruct((count, self.frames, rows, self.half), jnp.bfloat16)

    def call(self, steps, kernel, name, micros, in_specs, out_specs, out_shape, operands, params=PARAMS, aliases={}):
        return pl.pallas_call(
            kernel,
            grid_spec=pltpu.PrefetchScalarGridSpec(
                num_scalar_prefetch=1, grid=(steps,), in_specs=in_specs, out_specs=out_specs
            ),
            out_shape=out_shape,
            input_output_aliases=aliases,
            compiler_params=PARAMS,
        cost_estimate=cost(micros),
            name=name,
        )(self.place, *operands)

    def early_grads(self, swapped, same, other):
        return self.call(
            EARLY_STEPS,
            early_kernel,
            "temporal_early",
            EARLY_COST,
            [self.own(EARLY_STEPS, 0)] * 4
            + [self.part(EARLY_STEPS, 4, GROUP)]
            + [self.own(EARLY_STEPS, 1)] * 4
            + [self.part(EARLY_STEPS, 4, GROUP, 1)]
            + [self.part(EARLY_STEPS, 2, GROUP)] * 2,
            [self.part(EARLY_STEPS, 3, GROUP)] * 2
            + [self.part(EARLY_STEPS, 4, GROUP), self.stats()],
            [self.shape(3, GROUP)] * 2 + [self.shape(4, GROUP), self.stats_shape()],
            self.arrays + (swapped,) + self.arrays + (swapped, same, other),
        )

    def late_grads(self, swapped, same, other, far, *parts):
        out = pl.BlockSpec(
            (self.frames, self.positions, self.half // LATE_STEPS),
            lambda j, p: (0, 0, (p[0] % 2) * LATE_STEPS + j),
        )
        out_shape = jax.ShapeDtypeStruct((self.frames, self.positions, self.width), jnp.bfloat16)
        return self.call(
            LATE_STEPS,
            late_kernel,
            "temporal_late",
            LATE_COST,
            [self.own(LATE_STEPS, 1)] * 4
            + [self.part(LATE_STEPS, 4, GROUP, 1)]
            + [self.part(LATE_STEPS, 2, GROUP)] * 2
            + [self.stats()]
            + [self.part(LATE_STEPS, 3, GROUP)] * 2
            + [self.part(LATE_STEPS, 4, GROUP)],
            [out] * 3 + [self.part(LATE_STEPS, 3, self.positions)],
            [out_shape] * 3 + [self.shape(3, self.positions)],
            self.arrays + (swapped, same, other, far) + parts,
            LATE_PARAMS,
        )

    def finish(self, outs, swapped):
        out = pl.BlockSpec(
            (self.frames, self.positions, self.half // FINISH_STEPS),
            lambda j, p: (0, 0, (1 - p[0] % 2) * FINISH_STEPS + j),
        )
        return self.call(
            FINISH_STEPS,
            finish_kernel,
            "temporal_finish",
            3,
            [self.part(FINISH_STEPS, 3, self.positions)] + [pl.BlockSpec(memory_space=pl.ANY)] * 3,
            [out] * 3,
            [jax.ShapeDtypeStruct(a.shape, a.dtype) for a in outs],
            (swapped,) + tuple(outs),
            LATE_PARAMS,
            {2: 0, 3: 1, 4: 2},
        )


EARLY_COST = 100
LATE_COST = 100


def local(
    space_query, space_key, space_value, space_grad, time_query, time_key, time_value, time_grad
):
    def flat(array):
        return array.reshape(array.shape[1:])

    def chips(array):
        return lax.ppermute(array, "tm", CHIPS)

    def crossed(array):
        return lax.ppermute(array, "tm", CROSSED)

    def cores(array):
        return lax.ppermute(array, "tm", CORES)

    spatial = tuple(map(flat, (space_query, space_key, space_value, space_grad)))
    arrays = tuple(map(flat, (time_query, time_key, time_value, time_grad)))

    ships, arrays, spatial = lax.optimization_barrier((ship_pack(*arrays), arrays, spatial))
    same, other, swapped = chips(ships[0]), crossed(ships[1]), cores(ships[2])
    packed, swapped = lax.optimization_barrier((pack_heads(*spatial), swapped))
    packed = lax.all_to_all(packed, "space", 0, 0, tiled=True)
    work = Temporal(arrays)
    early, early_other, back, far = work.early_grads(swapped, same, other)
    far, back = chips(far), chips(back)
    packed = lax.all_to_all(spatial_grads(packed), "space", 0, 0, tiled=True)
    *outs, theirs = work.late_grads(swapped, same, other, far, early, early_other, back)
    outs = work.finish(outs, cores(theirs))
    outs = tuple(unpack_heads(packed)) + tuple(outs)
    return tuple(out.reshape(space_query.shape) for out in outs)


def solution(mesh):
    spec = P(None, "tm", "space", None)
    return jax.shard_map(
        local, mesh=mesh, in_specs=(spec,) * 8, out_specs=(spec,) * 6, check_vma=False
    )
```

```python
import math

import jax
import jax.numpy as jnp
from jax import lax
from jax.experimental import pallas as pl
from jax.experimental.pallas import tpu as pltpu
from jax.sharding import PartitionSpec as P

HEAD_DIM = 128
SCALE = 1.0 / math.sqrt(HEAD_DIM)
LOG2E = 1.0 / math.log(2.0)
MIB = 1024 * 1024
PARAMS = pltpu.CompilerParams(vmem_limit_bytes=60 * MIB)
LATE_PARAMS = pltpu.CompilerParams(vmem_limit_bytes=59 * MIB)
UNPACK_PARAMS = pltpu.CompilerParams(vmem_limit_bytes=16 * MIB)


def cost(micros):
    return pl.CostEstimate(flops=int(micros * 1e9), bytes_accessed=0, transcendentals=0)


def dot(a, b, contract):
    return lax.dot_general(a, b, (contract, ((), ())), preferred_element_type=jnp.float32)


def pack_kernel(*refs):
    *ins, out, rows, heads, row_sems, head_sems = refs
    count, frames = rows.shape[:2]

    def load(f, a):
        return pltpu.make_async_copy(ins[a].at[f], rows.at[a, f], row_sems.at[f, a])

    def store(f):
        return pltpu.make_async_copy(heads.at[:, f], out.at[:, f], head_sems.at[f])

    for f in range(frames):
        for a in range(count):
            load(f, a).start()
    for f in range(frames):
        for a in range(count):
            load(f, a).wait()
            for h in range(heads.shape[0]):
                heads[h, f, a] = rows[a, f, :, h * HEAD_DIM : (h + 1) * HEAD_DIM]
        store(f).start()
    for f in range(frames):
        store(f).wait()


def pack_heads(*arrays):
    frames, positions, width = arrays[0].shape
    count, heads = len(arrays), width // HEAD_DIM
    dtype = arrays[0].dtype
    packed = (heads, frames, count, positions, HEAD_DIM)
    return pl.pallas_call(
        pack_kernel,
        in_specs=[pl.BlockSpec(memory_space=pltpu.HBM)] * count,
        out_specs=pl.BlockSpec(memory_space=pl.ANY),
        out_shape=jax.ShapeDtypeStruct(packed, dtype),
        scratch_shapes=[
            pltpu.VMEM((count, frames, positions, width), dtype),
            pltpu.VMEM(packed, dtype),
            pltpu.SemaphoreType.DMA((frames, count)),
            pltpu.SemaphoreType.DMA((frames,)),
        ],
        compiler_params=PARAMS,
        cost_estimate=cost(5),
        name="pack_heads",
    )(*arrays)


def unpack_kernel(ref, *refs):
    *outs, rows, sems = refs
    count, frames = rows.shape[:2]
    copies = []
    for f in range(frames):
        for a in range(count):
            for h in range(ref.shape[0]):
                rows[a, f, :, h * HEAD_DIM : (h + 1) * HEAD_DIM] = ref[h, f, a]
            copies.append(pltpu.make_async_copy(rows.at[a, f], outs[a].at[f], sems.at[f, a]))
            copies[-1].start()
    for copy in copies:
        copy.wait()


def unpack_heads(array):
    heads, frames, count, positions, _ = array.shape
    shape = (frames, positions, heads * HEAD_DIM)
    return pl.pallas_call(
        unpack_kernel,
        in_specs=[pl.BlockSpec(memory_space=pltpu.VMEM)],
        out_specs=[pl.BlockSpec(memory_space=pltpu.HBM)] * count,
        out_shape=[jax.ShapeDtypeStruct(shape, array.dtype)] * count,
        scratch_shapes=[
            pltpu.VMEM((count,) + shape, array.dtype),
            pltpu.SemaphoreType.DMA((frames, count)),
        ],
        compiler_params=UNPACK_PARAMS,
        cost_estimate=cost(4),
        name="unpack_heads",
    )(array)


def spatial_kernel(ref, out):
    parts, _, _, rows, _ = ref.shape
    query, key, value, grad = (ref[:, 0, a].reshape(parts * rows, HEAD_DIM) for a in range(4))
    scores = dot(query, key, ((1,), (1,)))
    peak = jnp.max(scores, axis=1, keepdims=True)
    e = jnp.exp2((scores - peak) * (SCALE * LOG2E))
    pgrad = dot(grad, value, ((1,), (1,)))
    probs = e * (1.0 / jnp.sum(e, axis=1, keepdims=True))
    term = probs * pgrad
    delta = jnp.sum(term, axis=1, keepdims=True)
    sgrad = (term - probs * delta).astype(jnp.bfloat16)
    results = (
        dot(sgrad, key, ((1,), (0,))) * SCALE,
        dot(query.T, sgrad, ((1,), (0,))).T * SCALE,
        dot(grad.T, probs.astype(jnp.bfloat16), ((1,), (0,))).T,
    )
    for a, result in enumerate(results):
        out[:, 0, a] = result.astype(out.dtype).reshape(parts, rows, HEAD_DIM)


def spatial_grads(array):
    parts, frames, _, rows, _ = array.shape
    return pl.pallas_call(
        spatial_kernel,
        grid=(frames,),
        in_specs=[pl.BlockSpec((parts, 1, 4, rows, HEAD_DIM), lambda f: (0, f, 0, 0, 0))],
        out_specs=pl.BlockSpec((parts, 1, 3, rows, HEAD_DIM), lambda f: (0, f, 0, 0, 0)),
        out_shape=jax.ShapeDtypeStruct((parts, frames, 3, rows, HEAD_DIM), array.dtype),
        compiler_params=PARAMS,
        cost_estimate=cost(20),
        name="spatial_grads",
    )(array)


GROUP = 16
CHIPS = [(t, t ^ 2) for t in range(4)]
CORES = [(t, t ^ 1) for t in range(4)]
CROSSED = [(t, t ^ 3) for t in range(4)]
NEVER = -1e30


def copy_through(steps, sems, out_sems):
    loads = [
        pltpu.make_async_copy(source, middle, sems.at[i])
        for i, (source, middle, _) in enumerate(steps)
    ]
    stores = [
        pltpu.make_async_copy(middle, target, out_sems.at[i])
        for i, (_, middle, target) in enumerate(steps)
    ]
    for load in loads:
        load.start()
    for load, store in zip(loads, stores):
        load.wait()
        store.start()
    for store in stores:
        store.wait()


def half_columns(core, width):
    return pl.ds(pl.multiple_of(core * width, width), width)


def ship_kernel(query, key, value, grad, same, other, swap, held, held_swap, sems, out_sems):
    member = lax.axis_index("tm")
    chip, core = member // 2, member % 2
    width = same.shape[-1]
    own, others = half_columns(core, width), half_columns(1 - core, width)

    def copy_all(first, second, row):
        rows = pl.ds(row, GROUP)
        steps = [
            (ref.at[:, rows, columns], held.at[i, a], out.at[a])
            for i, (columns, out) in enumerate(((others, other), (own, same)))
            for a, ref in enumerate((first, second))
        ]
        steps += [
            (ref.at[:, :, others], held_swap.at[a], swap.at[a])
            for a, ref in enumerate((query, key, value, grad))
        ]
        copy_through(steps, sems, out_sems)

    @pl.when(chip == 0)
    def _():
        copy_all(key, value, 0)

    @pl.when(chip == 1)
    def _():
        copy_all(query, grad, GROUP)


def ship_pack(*arrays):
    frames, positions, width = arrays[0].shape
    dtype = arrays[0].dtype
    shape = jax.ShapeDtypeStruct((2, frames, GROUP, width // 2), dtype)
    swap_shape = jax.ShapeDtypeStruct((4, frames, positions, width // 2), dtype)
    hbm = pl.BlockSpec(memory_space=pltpu.HBM)
    return pl.pallas_call(
        ship_kernel,
        in_specs=[hbm] * 4,
        out_specs=[hbm] * 3,
        out_shape=[shape, shape, swap_shape],
        scratch_shapes=[
            pltpu.VMEM((2,) + shape.shape, dtype),
            pltpu.VMEM(swap_shape.shape, dtype),
            pltpu.SemaphoreType.DMA((8,)),
            pltpu.SemaphoreType.DMA((8,)),
        ],
        compiler_params=PARAMS,
        cost_estimate=cost(2),
        name="ship_pack",
    )(*arrays)


def frame_mask(core, chip_frames, causal):
    rows = chip_frames * GROUP
    half = chip_frames // 2
    key_row = lax.broadcasted_iota(jnp.int32, (rows, rows), 0)
    query_row = lax.broadcasted_iota(jnp.int32, (rows, rows), 1)
    same = key_row % GROUP == query_row % GROUP
    key_frame = (key_row // GROUP + core * half) % chip_frames
    query_frame = (query_row // GROUP + core * half) % chip_frames
    return same & ((key_frame <= query_frame) | jnp.logical_not(causal))


def gather_rows(own, other, row, columns):
    rows = pl.ds(row, GROUP)
    return jnp.concatenate(
        [
            own[:, rows, columns].reshape(-1, HEAD_DIM),
            other[:, rows, columns].reshape(-1, HEAD_DIM),
        ],
        axis=0,
    )


def block_stats(mask, query, key, value, grad):
    scores = dot(key, query, ((1,), (1,))) * (SCALE * LOG2E)
    scores = jnp.where(mask, scores, NEVER)
    peak = jnp.max(scores, axis=0, keepdims=True)
    e = jnp.exp2(scores - peak)
    pgrad = dot(value, grad, ((1,), (1,)))
    return (
        (scores, pgrad),
        (peak, jnp.sum(e, axis=0, keepdims=True), jnp.sum(e * pgrad, axis=0, keepdims=True)),
    )


def merged(stats, more):
    peak = jnp.maximum(stats[0], more[0])
    own_scale, more_scale = jnp.exp2(stats[0] - peak), jnp.exp2(more[0] - peak)
    inverse = 1.0 / (stats[1] * own_scale + more[1] * more_scale)
    return peak, inverse, (stats[2] * own_scale + more[2] * more_scale) * inverse


def block_weights(products, stats, more):
    scores, pgrad = products
    peak, inverse, delta = merged(stats, more)
    probs = jnp.exp2(scores - peak) * inverse
    return probs.astype(jnp.bfloat16), (probs * (pgrad - delta)).astype(jnp.bfloat16)


def block_grads(weights, sgrad, query, key, grad):
    dquery = dot(sgrad, key, ((0,), (0,))) * SCALE
    dkey = dot(sgrad, query, ((1,), (0,))) * SCALE
    dvalue = dot(weights, grad, ((1,), (0,)))
    return dquery, dkey, dvalue


def write_stats(out, h, heads, stats):
    for i, row in enumerate(stats):
        out[i, pl.ds(pl.program_id(0) * heads + h, 1)] = row


def read_stats(far, h, heads):
    return tuple(far[i, pl.ds(pl.program_id(0) * heads + h, 1)] for i in range(3))


def choose(first, when_first, when_second):
    return tuple(jnp.where(first, a, b) for a, b in zip(when_first, when_second))


def no_stats(rows):
    zero = jnp.zeros((1, rows), jnp.float32)
    return (zero + NEVER, zero, zero)


def place_rows(own, others, a, columns, values):
    values = values.astype(jnp.bfloat16).reshape(2, -1, GROUP, HEAD_DIM)
    own[a, :, :, columns] = values[0]
    others[a, :, :, columns] = values[1]


def load_rows(refs, swapped, columns):
    return [gather_rows(ref, swapped.at[a], 0, columns) for a, ref in enumerate(refs)]


def early_kernel(
    place, query, key, value, grad, swapped, late_query, late_key, late_value, late_grad,
    late_swapped, same, other, early, early_other, back, stats_out,
):
    core, first = place[0] % 2, place[0] < 2
    frames = query.shape[0]
    causal = frame_mask(core, 2 * frames, True)
    cross = frame_mask(core, 2 * frames, False)
    none = no_stats(2 * frames * GROUP)
    heads = query.shape[-1] // HEAD_DIM
    for h in range(heads):
        columns = pl.ds(h * HEAD_DIM, HEAD_DIM)
        rows = load_rows((query, key, value, grad), swapped, columns)
        late = load_rows((late_query, late_key, late_value, late_grad), late_swapped, columns)
        sent = [gather_rows(same.at[a], other.at[a], 0, columns) for a in range(2)]
        crossed = [
            jnp.where(first, sent[0], rows[0]),
            jnp.where(first, late[1], sent[0]),
            jnp.where(first, late[2], sent[1]),
            jnp.where(first, sent[1], rows[3]),
        ]
        products, stats = block_stats(causal, *rows)
        cross_products, cross_stats = block_stats(cross, *crossed)
        late_stats = block_stats(causal, *late)[1]
        write_stats(stats_out, h, heads, choose(first, cross_stats, late_stats))
        out = block_grads(
            *block_weights(products, stats, choose(first, none, cross_stats)),
            rows[0],
            rows[1],
            rows[3],
        )
        cross_weights, cross_sgrad = block_weights(
            cross_products, cross_stats, choose(first, none, stats)
        )
        cross_out = block_grads(cross_weights, cross_sgrad, crossed[0], crossed[1], crossed[3])
        mean_key = dot(cross_weights, crossed[1], ((0,), (0,))) * SCALE
        zero = jnp.zeros_like(mean_key)
        place_rows(early, early_other, 0, columns, out[0] + jnp.where(first, zero, cross_out[0]))
        place_rows(early, early_other, 1, columns, out[1])
        place_rows(early, early_other, 2, columns, out[2])
        returns = (
            jnp.where(first, cross_out[0], cross_out[1]),
            jnp.where(first, mean_key, cross_out[2]),
        )
        for a, values in enumerate(returns):
            place_rows(back.at[0:2], back.at[2:4], a, columns, values)


def late_kernel(
    place, query, key, value, grad, swapped, same, other, far, early, early_other, back,
    dquery, dkey, dvalue, theirs,
):
    core, first = place[0] % 2, place[0] < 2
    frames = query.shape[0]
    causal = frame_mask(core, 2 * frames, True)
    cross = frame_mask(core, 2 * frames, False)
    early_rows, late_rows = pl.ds(0, GROUP), pl.ds(GROUP, GROUP)
    none = no_stats(2 * frames * GROUP)
    heads = query.shape[-1] // HEAD_DIM
    for h in range(heads):
        columns = pl.ds(h * HEAD_DIM, HEAD_DIM)
        rows = load_rows((query, key, value, grad), swapped, columns)
        sent = [gather_rows(same.at[a], other.at[a], 0, columns) for a in range(2)]
        received = read_stats(far, h, heads)
        products, stats = block_stats(causal, *rows)
        more = choose(first, none, received)
        late = block_grads(*block_weights(products, stats, more), rows[0], rows[1], rows[3])

        cross_products, cross_stats = block_stats(cross, sent[0], rows[1], rows[2], sent[1])
        weights, sgrad = block_weights(cross_products, cross_stats, received)
        near_key = dot(sgrad, sent[0], ((1,), (0,))) * SCALE
        near_value = dot(weights, sent[1], ((1,), (0,)))

        peak, inverse, delta = merged(stats, received)
        share = received[1] * jnp.exp2(received[0] - peak) * inverse
        shift = share * (delta - received[2] / received[1])
        factors = jnp.concatenate(
            [share, shift, jnp.zeros((6, share.shape[1]), jnp.float32)], axis=0
        ).T
        far_rows = [
            jnp.concatenate(
                [back[side * 2 + a, :, :, columns].reshape(-1, HEAD_DIM) for side in range(2)],
                axis=0,
            ).astype(jnp.float32)
            for a in range(2)
        ]
        far_query = far_rows[0] * factors[:, 0:1] - far_rows[1] * factors[:, 1:2]
        zero = jnp.zeros_like(far_query)
        late = [
            late[0] + jnp.where(first, zero, far_query),
            late[1] + jnp.where(first, near_key, zero),
            late[2] + jnp.where(first, near_value, zero),
        ]
        late = [values.reshape(2, frames, GROUP, HEAD_DIM) for values in late]
        far_rows = [
            jnp.where(first, values, zero).reshape(2, frames, GROUP, HEAD_DIM)
            for values in far_rows
        ]

        def write(outs, side, early):
            for a, out in enumerate(outs):
                sums = early[a, :, :, columns].astype(jnp.float32)
                if a > 0:
                    sums += far_rows[a - 1][side]
                out[:, early_rows, columns] = sums.astype(jnp.bfloat16)
                out[:, late_rows, columns] = late[a][side].astype(jnp.bfloat16)

        write((dquery, dkey, dvalue), 0, early)
        write([theirs.at[a] for a in range(3)], 1, early_other)


def finish_kernel(place, swapped, *refs):
    for a, out in enumerate(refs[3:]):
        out[...] = swapped[a]


EARLY_STEPS, LATE_STEPS, FINISH_STEPS = 4, 4, 4


class Temporal:
    def __init__(self, arrays):
        self.arrays = arrays
        self.frames, self.positions, self.width = arrays[0].shape
        self.half = self.width // 2
        self.heads = self.half // HEAD_DIM
        member = lax.axis_index("tm")
        self.place = member.reshape(1)

    def own(self, steps, row):
        return pl.BlockSpec(
            (self.frames, GROUP, self.half // steps),
            lambda j, p: (0, row, (p[0] % 2) * steps + j),
        )

    def part(self, steps, count, rows, row=0):
        return pl.BlockSpec(
            (count, self.frames, rows, self.half // steps), lambda j, p: (0, 0, row, j)
        )

    def stats(self):
        return pl.BlockSpec(self.stats_shape().shape, lambda j, p: (0, 0, 0))

    def stats_shape(self):
        return jax.ShapeDtypeStruct((3, self.heads, 2 * self.frames * GROUP), jnp.float32)

    def shape(self, count, rows):
        return jax.ShapeDtypeStruct((count, self.frames, rows, self.half), jnp.bfloat16)

    def call(self, steps, kernel, name, micros, in_specs, out_specs, out_shape, operands, params=PARAMS, aliases={}):
        return pl.pallas_call(
            kernel,
            grid_spec=pltpu.PrefetchScalarGridSpec(
                num_scalar_prefetch=1, grid=(steps,), in_specs=in_specs, out_specs=out_specs
            ),
            out_shape=out_shape,
            input_output_aliases=aliases,
            compiler_params=PARAMS,
        cost_estimate=cost(micros),
            name=name,
        )(self.place, *operands)

    def early_grads(self, swapped, same, other):
        return self.call(
            EARLY_STEPS,
            early_kernel,
            "temporal_early",
            EARLY_COST,
            [self.own(EARLY_STEPS, 0)] * 4
            + [self.part(EARLY_STEPS, 4, GROUP)]
            + [self.own(EARLY_STEPS, 1)] * 4
            + [self.part(EARLY_STEPS, 4, GROUP, 1)]
            + [self.part(EARLY_STEPS, 2, GROUP)] * 2,
            [self.part(EARLY_STEPS, 3, GROUP)] * 2
            + [self.part(EARLY_STEPS, 4, GROUP), self.stats()],
            [self.shape(3, GROUP)] * 2 + [self.shape(4, GROUP), self.stats_shape()],
            self.arrays + (swapped,) + self.arrays + (swapped, same, other),
        )

    def late_grads(self, swapped, same, other, far, *parts):
        out = pl.BlockSpec(
            (self.frames, self.positions, self.half // LATE_STEPS),
            lambda j, p: (0, 0, (p[0] % 2) * LATE_STEPS + j),
        )
        out_shape = jax.ShapeDtypeStruct((self.frames, self.positions, self.width), jnp.bfloat16)
        return self.call(
            LATE_STEPS,
            late_kernel,
            "temporal_late",
            LATE_COST,
            [self.own(LATE_STEPS, 1)] * 4
            + [self.part(LATE_STEPS, 4, GROUP, 1)]
            + [self.part(LATE_STEPS, 2, GROUP)] * 2
            + [self.stats()]
            + [self.part(LATE_STEPS, 3, GROUP)] * 2
            + [self.part(LATE_STEPS, 4, GROUP)],
            [out] * 3 + [self.part(LATE_STEPS, 3, self.positions)],
            [out_shape] * 3 + [self.shape(3, self.positions)],
            self.arrays + (swapped, same, other, far) + parts,
            LATE_PARAMS,
        )

    def finish(self, outs, swapped):
        out = pl.BlockSpec(
            (self.frames, self.positions, self.half // FINISH_STEPS),
            lambda j, p: (0, 0, (1 - p[0] % 2) * FINISH_STEPS + j),
        )
        return self.call(
            FINISH_STEPS,
            finish_kernel,
            "temporal_finish",
            3,
            [self.part(FINISH_STEPS, 3, self.positions)] + [pl.BlockSpec(memory_space=pl.ANY)] * 3,
            [out] * 3,
            [jax.ShapeDtypeStruct(a.shape, a.dtype) for a in outs],
            (swapped,) + tuple(outs),
            LATE_PARAMS,
            {2: 0, 3: 1, 4: 2},
        )


EARLY_COST = 100
LATE_COST = 100


def exchange(array):
    members = lax.axis_size("space")
    groups = [[t * members + (i ^ (31 * (t % 2))) for i in range(members)] for t in range(4)]
    return lax.all_to_all(
        array, ("tm", "space"), 0, 0, axis_index_groups=groups, tiled=True
    )


def local(
    space_query, space_key, space_value, space_grad, time_query, time_key, time_value, time_grad
):
    def flat(array):
        return array.reshape(array.shape[1:])

    def chips(array):
        return lax.ppermute(array, "tm", CHIPS)

    def crossed(array):
        return lax.ppermute(array, "tm", CROSSED)

    def cores(array):
        return lax.ppermute(array, "tm", CORES)

    spatial = tuple(map(flat, (space_query, space_key, space_value, space_grad)))
    arrays = tuple(map(flat, (time_query, time_key, time_value, time_grad)))

    ships, arrays, spatial = lax.optimization_barrier((ship_pack(*arrays), arrays, spatial))
    same, other, swapped = chips(ships[0]), crossed(ships[1]), cores(ships[2])
    packed, swapped = lax.optimization_barrier((pack_heads(*spatial), swapped))
    packed = exchange(packed)
    work = Temporal(arrays)
    early, early_other, back, far = work.early_grads(swapped, same, other)
    far, back = chips(far), chips(back)
    packed = exchange(spatial_grads(packed))
    *outs, theirs = work.late_grads(swapped, same, other, far, early, early_other, back)
    outs = work.finish(outs, cores(theirs))
    outs = tuple(unpack_heads(packed)) + tuple(outs)
    return tuple(out.reshape(space_query.shape) for out in outs)


def solution(mesh):
    spec = P(None, "tm", "space", None)
    return jax.shard_map(
        local, mesh=mesh, in_specs=(spec,) * 8, out_specs=(spec,) * 6, check_vma=False
    )
```

```python
import math

import jax
import jax.numpy as jnp
from jax import lax
from jax.experimental import pallas as pl
from jax.experimental.pallas import tpu as pltpu
from jax.sharding import PartitionSpec as P

HEAD_DIM = 128
SCALE = 1.0 / math.sqrt(HEAD_DIM)
LOG2E = 1.0 / math.log(2.0)
MIB = 1024 * 1024
PARAMS = pltpu.CompilerParams(vmem_limit_bytes=60 * MIB)
LATE_PARAMS = pltpu.CompilerParams(vmem_limit_bytes=59 * MIB)
UNPACK_PARAMS = pltpu.CompilerParams(vmem_limit_bytes=16 * MIB)


def cost(micros):
    return pl.CostEstimate(flops=int(micros * 1e9), bytes_accessed=0, transcendentals=0)


def dot(a, b, contract):
    return lax.dot_general(a, b, (contract, ((), ())), preferred_element_type=jnp.float32)


def pack_kernel(*refs):
    *ins, out, rows, heads, row_sems, head_sems = refs
    count, frames = rows.shape[:2]

    def load(f, a):
        return pltpu.make_async_copy(ins[a].at[f], rows.at[a, f], row_sems.at[f, a])

    def store(f):
        return pltpu.make_async_copy(heads.at[:, f], out.at[:, f], head_sems.at[f])

    for f in range(frames):
        for a in range(count):
            load(f, a).start()
    for f in range(frames):
        for a in range(count):
            load(f, a).wait()
            for h in range(heads.shape[0]):
                heads[h, f, a] = rows[a, f, :, h * HEAD_DIM : (h + 1) * HEAD_DIM]
        store(f).start()
    for f in range(frames):
        store(f).wait()


def pack_heads(*arrays):
    frames, positions, width = arrays[0].shape
    count, heads = len(arrays), width // HEAD_DIM
    dtype = arrays[0].dtype
    packed = (heads, frames, count, positions, HEAD_DIM)
    return pl.pallas_call(
        pack_kernel,
        in_specs=[pl.BlockSpec(memory_space=pltpu.HBM)] * count,
        out_specs=pl.BlockSpec(memory_space=pl.ANY),
        out_shape=jax.ShapeDtypeStruct(packed, dtype),
        scratch_shapes=[
            pltpu.VMEM((count, frames, positions, width), dtype),
            pltpu.VMEM(packed, dtype),
            pltpu.SemaphoreType.DMA((frames, count)),
            pltpu.SemaphoreType.DMA((frames,)),
        ],
        compiler_params=PARAMS,
        cost_estimate=cost(5),
        name="pack_heads",
    )(*arrays)


def unpack_kernel(ref, *refs):
    *outs, rows, sems = refs
    count, frames = rows.shape[:2]
    copies = []
    for f in range(frames):
        for a in range(count):
            for h in range(ref.shape[0]):
                rows[a, f, :, h * HEAD_DIM : (h + 1) * HEAD_DIM] = ref[h, f, a]
            copies.append(pltpu.make_async_copy(rows.at[a, f], outs[a].at[f], sems.at[f, a]))
            copies[-1].start()
    for copy in copies:
        copy.wait()


def unpack_heads(array):
    heads, frames, count, positions, _ = array.shape
    shape = (frames, positions, heads * HEAD_DIM)
    return pl.pallas_call(
        unpack_kernel,
        in_specs=[pl.BlockSpec(memory_space=pltpu.VMEM)],
        out_specs=[pl.BlockSpec(memory_space=pltpu.HBM)] * count,
        out_shape=[jax.ShapeDtypeStruct(shape, array.dtype)] * count,
        scratch_shapes=[
            pltpu.VMEM((count,) + shape, array.dtype),
            pltpu.SemaphoreType.DMA((frames, count)),
        ],
        compiler_params=UNPACK_PARAMS,
        cost_estimate=cost(4),
        name="unpack_heads",
    )(array)


def spatial_kernel(ref, out):
    parts, _, _, rows, _ = ref.shape
    query, key, value, grad = (ref[:, 0, a].reshape(parts * rows, HEAD_DIM) for a in range(4))
    scores = dot(query, key, ((1,), (1,)))
    peak = jnp.max(scores, axis=1, keepdims=True)
    e = jnp.exp2((scores - peak) * (SCALE * LOG2E))
    pgrad = dot(grad, value, ((1,), (1,)))
    probs = e * (1.0 / jnp.sum(e, axis=1, keepdims=True))
    term = probs * pgrad
    delta = jnp.sum(term, axis=1, keepdims=True)
    sgrad = (term - probs * delta).astype(jnp.bfloat16)
    results = (
        dot(sgrad, key, ((1,), (0,))) * SCALE,
        dot(query.T, sgrad, ((1,), (0,))).T * SCALE,
        dot(grad.T, probs.astype(jnp.bfloat16), ((1,), (0,))).T,
    )
    for a, result in enumerate(results):
        out[:, 0, a] = result.astype(out.dtype).reshape(parts, rows, HEAD_DIM)


def spatial_grads(array):
    parts, frames, _, rows, _ = array.shape
    return pl.pallas_call(
        spatial_kernel,
        grid=(frames,),
        in_specs=[pl.BlockSpec((parts, 1, 4, rows, HEAD_DIM), lambda f: (0, f, 0, 0, 0))],
        out_specs=pl.BlockSpec((parts, 1, 3, rows, HEAD_DIM), lambda f: (0, f, 0, 0, 0)),
        out_shape=jax.ShapeDtypeStruct((parts, frames, 3, rows, HEAD_DIM), array.dtype),
        compiler_params=PARAMS,
        cost_estimate=cost(20),
        name="spatial_grads",
    )(array)


GROUP = 16
CHIPS = [(t, t ^ 2) for t in range(4)]
CORES = [(t, t ^ 1) for t in range(4)]
CROSSED = [(t, t ^ 3) for t in range(4)]
NEVER = -1e30


def copy_through(steps, sems, out_sems):
    loads = [
        pltpu.make_async_copy(source, middle, sems.at[i])
        for i, (source, middle, _) in enumerate(steps)
    ]
    stores = [
        pltpu.make_async_copy(middle, target, out_sems.at[i])
        for i, (_, middle, target) in enumerate(steps)
    ]
    for load in loads:
        load.start()
    for load, store in zip(loads, stores):
        load.wait()
        store.start()
    for store in stores:
        store.wait()


def half_columns(core, width):
    return pl.ds(pl.multiple_of(core * width, width), width)


def ship_kernel(query, key, value, grad, same, other, swap, held, held_swap, sems, out_sems):
    member = lax.axis_index("tm")
    chip, core = member // 2, member % 2
    width = same.shape[-1]
    own, others = half_columns(core, width), half_columns(1 - core, width)

    def copy_all(first, second, row):
        rows = pl.ds(row, GROUP)
        steps = [
            (ref.at[:, rows, columns], held.at[i, a], out.at[a])
            for i, (columns, out) in enumerate(((others, other), (own, same)))
            for a, ref in enumerate((first, second))
        ]
        steps += [
            (ref.at[:, :, others], held_swap.at[a], swap.at[a])
            for a, ref in enumerate((query, key, value, grad))
        ]
        copy_through(steps, sems, out_sems)

    @pl.when(chip == 0)
    def _():
        copy_all(key, value, 0)

    @pl.when(chip == 1)
    def _():
        copy_all(query, grad, GROUP)


def ship_pack(*arrays):
    frames, positions, width = arrays[0].shape
    dtype = arrays[0].dtype
    shape = jax.ShapeDtypeStruct((2, frames, GROUP, width // 2), dtype)
    swap_shape = jax.ShapeDtypeStruct((4, frames, positions, width // 2), dtype)
    hbm = pl.BlockSpec(memory_space=pltpu.HBM)
    return pl.pallas_call(
        ship_kernel,
        in_specs=[hbm] * 4,
        out_specs=[hbm] * 3,
        out_shape=[shape, shape, swap_shape],
        scratch_shapes=[
            pltpu.VMEM((2,) + shape.shape, dtype),
            pltpu.VMEM(swap_shape.shape, dtype),
            pltpu.SemaphoreType.DMA((8,)),
            pltpu.SemaphoreType.DMA((8,)),
        ],
        compiler_params=PARAMS,
        cost_estimate=cost(2),
        name="ship_pack",
    )(*arrays)


def frame_mask(core, chip_frames, causal):
    rows = chip_frames * GROUP
    half = chip_frames // 2
    key_row = lax.broadcasted_iota(jnp.int32, (rows, rows), 0)
    query_row = lax.broadcasted_iota(jnp.int32, (rows, rows), 1)
    same = key_row % GROUP == query_row % GROUP
    key_frame = (key_row // GROUP + core * half) % chip_frames
    query_frame = (query_row // GROUP + core * half) % chip_frames
    return same & ((key_frame <= query_frame) | jnp.logical_not(causal))


def gather_rows(own, other, row, columns):
    rows = pl.ds(row, GROUP)
    return jnp.concatenate(
        [
            own[:, rows, columns].reshape(-1, HEAD_DIM),
            other[:, rows, columns].reshape(-1, HEAD_DIM),
        ],
        axis=0,
    )


def block_stats(mask, query, key, value, grad):
    scores = dot(key, query, ((1,), (1,))) * (SCALE * LOG2E)
    scores = jnp.where(mask, scores, NEVER)
    peak = jnp.max(scores, axis=0, keepdims=True)
    e = jnp.exp2(scores - peak)
    pgrad = dot(value, grad, ((1,), (1,)))
    return (
        (scores, pgrad),
        (peak, jnp.sum(e, axis=0, keepdims=True), jnp.sum(e * pgrad, axis=0, keepdims=True)),
    )


def merged(stats, more):
    peak = jnp.maximum(stats[0], more[0])
    own_scale, more_scale = jnp.exp2(stats[0] - peak), jnp.exp2(more[0] - peak)
    inverse = 1.0 / (stats[1] * own_scale + more[1] * more_scale)
    return peak, inverse, (stats[2] * own_scale + more[2] * more_scale) * inverse


def block_weights(products, stats, more):
    scores, pgrad = products
    peak, inverse, delta = merged(stats, more)
    probs = jnp.exp2(scores - peak) * inverse
    return probs.astype(jnp.bfloat16), (probs * (pgrad - delta)).astype(jnp.bfloat16)


def block_grads(weights, sgrad, query, key, grad):
    dquery = dot(sgrad, key, ((0,), (0,))) * SCALE
    dkey = dot(sgrad, query, ((1,), (0,))) * SCALE
    dvalue = dot(weights, grad, ((1,), (0,)))
    return dquery, dkey, dvalue


def write_stats(out, h, heads, stats):
    for i, row in enumerate(stats):
        out[i, pl.ds(pl.program_id(0) * heads + h, 1)] = row


def read_stats(far, h, heads):
    return tuple(far[i, pl.ds(pl.program_id(0) * heads + h, 1)] for i in range(3))


def choose(first, when_first, when_second):
    return tuple(jnp.where(first, a, b) for a, b in zip(when_first, when_second))


def no_stats(rows):
    zero = jnp.zeros((1, rows), jnp.float32)
    return (zero + NEVER, zero, zero)


def place_rows(own, others, a, columns, values):
    values = values.astype(jnp.bfloat16).reshape(2, -1, GROUP, HEAD_DIM)
    own[a, :, :, columns] = values[0]
    others[a, :, :, columns] = values[1]


def load_rows(refs, swapped, columns):
    return [gather_rows(ref, swapped.at[a], 0, columns) for a, ref in enumerate(refs)]


def early_kernel(
    place, query, key, value, grad, swapped, late_query, late_key, late_value, late_grad,
    late_swapped, same, other, early, early_other, back, stats_out,
):
    core, first = place[0] % 2, place[0] < 2
    frames = query.shape[0]
    causal = frame_mask(core, 2 * frames, True)
    cross = frame_mask(core, 2 * frames, False)
    none = no_stats(2 * frames * GROUP)
    heads = query.shape[-1] // HEAD_DIM
    for h in range(heads):
        columns = pl.ds(h * HEAD_DIM, HEAD_DIM)
        rows = load_rows((query, key, value, grad), swapped, columns)
        late = load_rows((late_query, late_key, late_value, late_grad), late_swapped, columns)
        sent = [gather_rows(same.at[a], other.at[a], 0, columns) for a in range(2)]
        crossed = [
            jnp.where(first, sent[0], rows[0]),
            jnp.where(first, late[1], sent[0]),
            jnp.where(first, late[2], sent[1]),
            jnp.where(first, sent[1], rows[3]),
        ]
        products, stats = block_stats(causal, *rows)
        cross_products, cross_stats = block_stats(cross, *crossed)
        late_stats = block_stats(causal, *late)[1]
        write_stats(stats_out, h, heads, choose(first, cross_stats, late_stats))
        out = block_grads(
            *block_weights(products, stats, choose(first, none, cross_stats)),
            rows[0],
            rows[1],
            rows[3],
        )
        cross_weights, cross_sgrad = block_weights(
            cross_products, cross_stats, choose(first, none, stats)
        )
        cross_out = block_grads(cross_weights, cross_sgrad, crossed[0], crossed[1], crossed[3])
        mean_key = dot(cross_weights, crossed[1], ((0,), (0,))) * SCALE
        zero = jnp.zeros_like(mean_key)
        place_rows(early, early_other, 0, columns, out[0] + jnp.where(first, zero, cross_out[0]))
        place_rows(early, early_other, 1, columns, out[1])
        place_rows(early, early_other, 2, columns, out[2])
        returns = (
            jnp.where(first, cross_out[0], cross_out[1]),
            jnp.where(first, mean_key, cross_out[2]),
        )
        for a, values in enumerate(returns):
            place_rows(back.at[0:2], back.at[2:4], a, columns, values)


def late_kernel(
    place, query, key, value, grad, swapped, same, other, far, early, early_other, back,
    dquery, dkey, dvalue, theirs,
):
    core, first = place[0] % 2, place[0] < 2
    frames = query.shape[0]
    causal = frame_mask(core, 2 * frames, True)
    cross = frame_mask(core, 2 * frames, False)
    early_rows, late_rows = pl.ds(0, GROUP), pl.ds(GROUP, GROUP)
    none = no_stats(2 * frames * GROUP)
    heads = query.shape[-1] // HEAD_DIM
    for h in range(heads):
        columns = pl.ds(h * HEAD_DIM, HEAD_DIM)
        rows = load_rows((query, key, value, grad), swapped, columns)
        sent = [gather_rows(same.at[a], other.at[a], 0, columns) for a in range(2)]
        received = read_stats(far, h, heads)
        products, stats = block_stats(causal, *rows)
        more = choose(first, none, received)
        late = block_grads(*block_weights(products, stats, more), rows[0], rows[1], rows[3])

        cross_products, cross_stats = block_stats(cross, sent[0], rows[1], rows[2], sent[1])
        weights, sgrad = block_weights(cross_products, cross_stats, received)
        near_key = dot(sgrad, sent[0], ((1,), (0,))) * SCALE
        near_value = dot(weights, sent[1], ((1,), (0,)))

        peak, inverse, delta = merged(stats, received)
        share = received[1] * jnp.exp2(received[0] - peak) * inverse
        shift = share * (delta - received[2] / received[1])
        factors = jnp.concatenate(
            [share, shift, jnp.zeros((6, share.shape[1]), jnp.float32)], axis=0
        ).T
        far_rows = [
            jnp.concatenate(
                [back[side * 2 + a, :, :, columns].reshape(-1, HEAD_DIM) for side in range(2)],
                axis=0,
            ).astype(jnp.float32)
            for a in range(2)
        ]
        far_query = far_rows[0] * factors[:, 0:1] - far_rows[1] * factors[:, 1:2]
        zero = jnp.zeros_like(far_query)
        late = [
            late[0] + jnp.where(first, zero, far_query),
            late[1] + jnp.where(first, near_key, zero),
            late[2] + jnp.where(first, near_value, zero),
        ]
        late = [values.reshape(2, frames, GROUP, HEAD_DIM) for values in late]
        far_rows = [
            jnp.where(first, values, zero).reshape(2, frames, GROUP, HEAD_DIM)
            for values in far_rows
        ]

        def write(outs, side, early):
            for a, out in enumerate(outs):
                sums = early[a, :, :, columns].astype(jnp.float32)
                if a > 0:
                    sums += far_rows[a - 1][side]
                out[:, early_rows, columns] = sums.astype(jnp.bfloat16)
                out[:, late_rows, columns] = late[a][side].astype(jnp.bfloat16)

        write((dquery, dkey, dvalue), 0, early)
        write([theirs.at[a] for a in range(3)], 1, early_other)


def finish_kernel(place, swapped, *refs):
    for a, out in enumerate(refs[3:]):
        out[...] = swapped[a]


EARLY_STEPS, LATE_STEPS, FINISH_STEPS = 4, 4, 4


class Temporal:
    def __init__(self, arrays):
        self.arrays = arrays
        self.frames, self.positions, self.width = arrays[0].shape
        self.half = self.width // 2
        self.heads = self.half // HEAD_DIM
        member = lax.axis_index("tm")
        self.place = member.reshape(1)

    def own(self, steps, row):
        return pl.BlockSpec(
            (self.frames, GROUP, self.half // steps),
            lambda j, p: (0, row, (p[0] % 2) * steps + j),
        )

    def part(self, steps, count, rows, row=0):
        return pl.BlockSpec(
            (count, self.frames, rows, self.half // steps), lambda j, p: (0, 0, row, j)
        )

    def stats(self):
        return pl.BlockSpec(self.stats_shape().shape, lambda j, p: (0, 0, 0))

    def stats_shape(self):
        return jax.ShapeDtypeStruct((3, self.heads, 2 * self.frames * GROUP), jnp.float32)

    def shape(self, count, rows):
        return jax.ShapeDtypeStruct((count, self.frames, rows, self.half), jnp.bfloat16)

    def call(self, steps, kernel, name, micros, in_specs, out_specs, out_shape, operands, params=PARAMS, aliases={}):
        return pl.pallas_call(
            kernel,
            grid_spec=pltpu.PrefetchScalarGridSpec(
                num_scalar_prefetch=1, grid=(steps,), in_specs=in_specs, out_specs=out_specs
            ),
            out_shape=out_shape,
            input_output_aliases=aliases,
            compiler_params=PARAMS,
        cost_estimate=cost(micros),
            name=name,
        )(self.place, *operands)

    def early_grads(self, swapped, same, other):
        return self.call(
            EARLY_STEPS,
            early_kernel,
            "temporal_early",
            EARLY_COST,
            [self.own(EARLY_STEPS, 0)] * 4
            + [self.part(EARLY_STEPS, 4, GROUP)]
            + [self.own(EARLY_STEPS, 1)] * 4
            + [self.part(EARLY_STEPS, 4, GROUP, 1)]
            + [self.part(EARLY_STEPS, 2, GROUP)] * 2,
            [self.part(EARLY_STEPS, 3, GROUP)] * 2
            + [self.part(EARLY_STEPS, 4, GROUP), self.stats()],
            [self.shape(3, GROUP)] * 2 + [self.shape(4, GROUP), self.stats_shape()],
            self.arrays + (swapped,) + self.arrays + (swapped, same, other),
        )

    def late_grads(self, swapped, same, other, far, *parts):
        out = pl.BlockSpec(
            (self.frames, self.positions, self.half // LATE_STEPS),
            lambda j, p: (0, 0, (p[0] % 2) * LATE_STEPS + j),
        )
        out_shape = jax.ShapeDtypeStruct((self.frames, self.positions, self.width), jnp.bfloat16)
        return self.call(
            LATE_STEPS,
            late_kernel,
            "temporal_late",
            LATE_COST,
            [self.own(LATE_STEPS, 1)] * 4
            + [self.part(LATE_STEPS, 4, GROUP, 1)]
            + [self.part(LATE_STEPS, 2, GROUP)] * 2
            + [self.stats()]
            + [self.part(LATE_STEPS, 3, GROUP)] * 2
            + [self.part(LATE_STEPS, 4, GROUP)],
            [out] * 3 + [self.part(LATE_STEPS, 3, self.positions)],
            [out_shape] * 3 + [self.shape(3, self.positions)],
            self.arrays + (swapped, same, other, far) + parts,
            LATE_PARAMS,
        )

    def finish(self, outs, swapped):
        out = pl.BlockSpec(
            (self.frames, self.positions, self.half // FINISH_STEPS),
            lambda j, p: (0, 0, (1 - p[0] % 2) * FINISH_STEPS + j),
        )
        return self.call(
            FINISH_STEPS,
            finish_kernel,
            "temporal_finish",
            3,
            [self.part(FINISH_STEPS, 3, self.positions)] + [pl.BlockSpec(memory_space=pl.ANY)] * 3,
            [out] * 3,
            [jax.ShapeDtypeStruct(a.shape, a.dtype) for a in outs],
            (swapped,) + tuple(outs),
            LATE_PARAMS,
            {2: 0, 3: 1, 4: 2},
        )


EARLY_COST = 100
LATE_COST = 100


def exchange(array):
    members = lax.axis_size("space")
    groups = [[t * members + (i ^ (31 * (t % 2)) ^ (16 * (t // 2))) for i in range(members)] for t in range(4)]
    return lax.all_to_all(
        array, ("tm", "space"), 0, 0, axis_index_groups=groups, tiled=True
    )


def local(
    space_query, space_key, space_value, space_grad, time_query, time_key, time_value, time_grad
):
    def flat(array):
        return array.reshape(array.shape[1:])

    def chips(array):
        return lax.ppermute(array, "tm", CHIPS)

    def crossed(array):
        return lax.ppermute(array, "tm", CROSSED)

    def cores(array):
        return lax.ppermute(array, "tm", CORES)

    spatial = tuple(map(flat, (space_query, space_key, space_value, space_grad)))
    arrays = tuple(map(flat, (time_query, time_key, time_value, time_grad)))

    ships, arrays, spatial = lax.optimization_barrier((ship_pack(*arrays), arrays, spatial))
    same, other, swapped = chips(ships[0]), crossed(ships[1]), cores(ships[2])
    packed, swapped = lax.optimization_barrier((pack_heads(*spatial), swapped))
    packed = exchange(packed)
    work = Temporal(arrays)
    early, early_other, back, far = work.early_grads(swapped, same, other)
    far, back = chips(far), chips(back)
    packed = exchange(spatial_grads(packed))
    *outs, theirs = work.late_grads(swapped, same, other, far, early, early_other, back)
    outs = work.finish(outs, cores(theirs))
    outs = tuple(unpack_heads(packed)) + tuple(outs)
    return tuple(out.reshape(space_query.shape) for out in outs)


def solution(mesh):
    spec = P(None, "tm", "space", None)
    return jax.shard_map(
        local, mesh=mesh, in_specs=(spec,) * 8, out_specs=(spec,) * 6, check_vma=False
    )
```
